128 devices in a mesh: ctx: 16 (over y, z), exp: 8 (over x, core).
Axes of the slice: x: 4, y: 4, z: 4, core: 2. Of those that a mesh axis runs over, the one named last changes fastest.
Arguments:
- query_rows: bfloat16 [2048, 8192], P('ctx', 'exp'), may hold values from -6 to 6
- key_rows: bfloat16 [2048, 8192], P('ctx', 'exp'), may hold values from -6 to 6
- value_rows: bfloat16 [2048, 8192], P('ctx', 'exp'), may hold values from -6 to 6
- log_decay: float32 [64, 2048], P('exp', 'ctx'), may hold values from -2.2 to 0, as said below
- residual: bfloat16 [2048, 6144], P('ctx', 'exp'), may hold values from -6 to 6
- out_weight: bfloat16 [8192, 6144], P('exp', 'ctx'), may hold values from -0.0625 to 0.0625
- router_weight: bfloat16 [6144, 8], replicated, may hold values from -0.0390625 to 0.0390625
- expert_ids: int32 [2048, 2], P('ctx'), may hold values from 0 to 7, all different within a row; in each aligned block of 128 rows (0 to 127, 128 to 255, ...) at most 36 rows name the same one
- expert_gate: bfloat16 [8, 6144, 9216], P('exp', None, 'ctx'), may hold values from -0.078125 to 0.078125
- expert_up: bfloat16 [8, 6144, 9216], P('exp', None, 'ctx'), may hold values from -0.078125 to 0.078125
- expert_down: bfloat16 [8, 9216, 6144], P('exp', 'ctx'), may hold values from -0.0625 to 0.0625
Outputs:
- hidden: bfloat16 [2048, 6144], P('ctx', 'exp')
- mixture: bfloat16 [2048, 6144], P('ctx', 'exp')
The draws below stay inside these ranges and needn't reach their ends.
Inputs may be any that keep to these rules, and one draw needn't show every extreme that they name: `expert_ids`: the two ids of a row differ. In each aligned block of 128 rows (the rows of one device along ctx) no expert is named by more than 36 rows, and in some block an expert is named by exactly 36 rows. `log_decay`: every entry is negative.
All inputs are finite; a program needn't handle non-finite values.
Results may differ from the reference program's by a relative error of at most 0.035.
Values may be sent and summed in bfloat16 or wider, within the bound.
A program may use at most 128 MiB of HBM per device.

```python
import math
import jax
import jax.numpy as jnp
import numpy as np
from jax import lax

D = 6144
HEAD_TOTAL = 64
HEAD_SIZE = 128
FF = 9216
TOK_DEV = 128
TOKEN_TOTAL = 2048
EXPERTS = 8
CAP = 36
QD = 8192
N_CTX = 16


def draw_log_decay(key, part):
    key = jax.random.fold_in(key, 11)
    pick_key, fast_key, slow_key, rough_key, location_random_key, depth_random_key = jax.random.split(key, 6)
    fast_share = 0.5
    chosen = jax.random.uniform(pick_key, (HEAD_TOTAL,)) < fast_share
    fast_rate = jnp.exp(jax.random.uniform(fast_key, (HEAD_TOTAL,), minval=jnp.log(1.0 / 50.0), maxval=jnp.log(1.0 / 30.0)))
    slow_rate = jnp.exp(jax.random.uniform(slow_key, (HEAD_TOTAL,), minval=jnp.log(0.01), maxval=jnp.log(0.1))) / TOKEN_TOTAL
    decay_speed = jnp.where(chosen, fast_rate, slow_rate)
    jaggedness = jax.random.uniform(rough_key, (HEAD_TOTAL, TOKEN_TOTAL), minval=0.5, maxval=1.5)
    spike_location = jax.random.randint(location_random_key, (HEAD_TOTAL, 3), 0, TOKEN_TOTAL)
    spike_depth = jax.random.uniform(depth_random_key, (HEAD_TOTAL, 3), minval=0.22, maxval=0.69)
    token_position = jnp.arange(TOKEN_TOTAL, dtype=jnp.int32)
    spike_tokens = jnp.sum(jnp.where(token_position[None, None, :] == spike_location[:, :, None], spike_depth[:, :, None], 0.0), axis=1)
    return -(decay_speed[:, None] * jaggedness + spike_tokens)


def shard_levels(stream_key, dims, cuts, low, largest):
    factor_of = 1.0
    for dim, blocks in cuts:
        draws = jax.random.uniform(jax.random.fold_in(jax.random.fold_in(stream_key, 6), dim), (blocks,), jnp.float32, low / len(cuts), largest / len(cuts))
        factor_of = factor_of * jnp.repeat(jnp.exp(draws), dims[dim] // blocks).reshape((-1,) + (1,) * (len(dims) - 1 - dim))
    return factor_of


def assign_block(own_key, own, number, rows, amount, top, bound, slope):
    sequence = jax.random.permutation(own_key, amount)
    heavy_load, ordinary = portions_of(amount, rows * top, bound, slope, True), portions_of(amount, rows * top, bound, slope, False)
    places = jnp.arange(amount)

    def named(sizes, rotation):
        used = int((sizes > 0).sum())
        fixed = max(1, used // 4)
        passed = fixed + (places - fixed + rotation * (used - fixed)) % max(1, amount - fixed)
        return jnp.zeros((amount,), jnp.int32).at[sequence[jnp.where(places < fixed, places, passed)]].set(jnp.asarray(sizes, jnp.int32))

    sizes = jnp.where(number % 4 == 0, named(heavy_load, number // 4), named(ordinary, number - number // 4 - 1))
    mixed = jax.random.permutation(jax.random.fold_in(own, 3), amount)
    source_of, sink = mixed[0:amount // 2 * 2:2], mixed[1:amount // 2 * 2:2]
    room = jnp.minimum(sizes[source_of] - 1, bound - sizes[sink]) // 2
    room = jnp.where((source_of == sequence[0]) | (sink == sequence[0]) | (sizes[sink] == 0), 0, jnp.maximum(room, 0))
    passed = jax.random.randint(jax.random.fold_in(own, 4), (amount // 2,), 0, 1 << 20) % (room + 1)
    sizes = sizes.at[source_of].add(-passed).at[sink].add(passed)
    labels = jnp.searchsorted(jnp.cumsum(sizes), jnp.arange(rows * top), side="right").astype(jnp.int32)
    grid = labels.reshape(top, rows).T
    grid = grid[jax.random.permutation(jax.random.fold_in(own, 1), rows)]
    rotation = jax.random.randint(jax.random.fold_in(own, 2), (rows, 1), 0, top)
    return jnp.take_along_axis(grid, (jnp.arange(top)[None, :] + rotation) % top, axis=1)


def portions_of(count, total, most, lean, full):
    loads = [(1 << 20) // math.isqrt(standing ** lean) + 1 for standing in range(1, count + 1)]
    largest = most if full else min(most, max(-(-total // count), total * loads[0] // sum(loads)))
    least = 1 if total - largest >= count - 1 else 0
    given, spare = [largest] + [least] * (count - 1), total - largest - least * (count - 1)
    while spare > 0:
        movable = [i for i in range(1, count) if given[i] < largest] or [i for i in range(1, count) if given[i] < most]
        mass, budget = sum([loads[i] for i in movable]), spare
        for i in movable:
            more = min(most - given[i], max(1, budget * loads[i] // mass), spare)
            given[i] = given[i] + more
            spare = spare - more
    return np.array(given)


def noise(key, shape, scale, bound, cuts=(), kind=jnp.bfloat16):
    loudness = shard_levels(key, shape, cuts, -0.22, 0.18) if cuts else 1.0
    values = jax.random.normal(key, shape, jnp.float32) * scale * loudness
    return jnp.minimum(jnp.maximum(values, -bound), bound).astype(kind)


def setup_inputs(seed: int = 0) -> dict:
    arg_keys = jax.random.split(jax.random.key(seed), 12)
    query_rows = noise(arg_keys[0], (TOKEN_TOTAL, QD), 1.0, 6.0, ((0, 16), (1, 8)))
    key_rows = noise(arg_keys[1], (TOKEN_TOTAL, QD), 1.0, 6.0, ((0, 16), (1, 8)))
    value_rows = noise(arg_keys[2], (TOKEN_TOTAL, QD), 1.0, 6.0, ((0, 16), (1, 8)))
    log_decay = draw_log_decay(jax.random.fold_in(arg_keys[11], 71), 0)
    residual = noise(arg_keys[4], (TOKEN_TOTAL, D), 1.0, 6.0, ((0, 16), (1, 8)))
    out_weight = noise(arg_keys[5], (QD, D), QD ** -0.5, 0.0625, ((0, 8), (1, 16)))
    router_weight = noise(arg_keys[6], (D, EXPERTS), (4 * D) ** -0.5, 0.0390625)
    expert_ids_keys = jax.random.split(jax.random.fold_in(arg_keys[7], 1), TOKEN_TOTAL // TOK_DEV)
    expert_ids_turns = jax.random.permutation(jax.random.fold_in(arg_keys[7], 3), TOKEN_TOTAL // TOK_DEV)
    expert_ids = jax.vmap(lambda own, number: assign_block(jax.random.fold_in(arg_keys[7], 2), own, number, TOK_DEV, EXPERTS, 2, CAP, 0))(expert_ids_keys, expert_ids_turns).reshape((TOKEN_TOTAL, 2))
    expert_gate = noise(arg_keys[8], (EXPERTS, D, FF), D ** -0.5, 0.078125, ((0, 8), (2, 16)))
    expert_up = noise(arg_keys[9], (EXPERTS, D, FF), D ** -0.5, 0.078125, ((0, 8), (2, 16)))
    expert_down = noise(arg_keys[10], (EXPERTS, FF, D), FF ** -0.5, 0.0625, ((0, 8), (1, 16)))
    return dict(query_rows=query_rows, key_rows=key_rows, value_rows=value_rows, log_decay=log_decay, residual=residual, out_weight=out_weight, router_weight=router_weight, expert_ids=expert_ids, expert_gate=expert_gate, expert_up=expert_up, expert_down=expert_down)


epsilon = 1e-05
highest = lax.Precision.HIGHEST

def attend_block(prior_state, bundle):
    query_blk, key_blk, value_blk, decay_blk = bundle
    cumulative = jnp.cumsum(decay_blk, axis=1)
    width = decay_blk.shape[1]
    row_index = lax.broadcasted_iota(jnp.int32, (width, width), 0)
    col_index = lax.broadcasted_iota(jnp.int32, (width, width), 1)
    gaps = cumulative[:, :, None] - cumulative[:, None, :]
    mask_weights = jnp.where((col_index <= row_index)[None], jnp.exp(jnp.minimum(gaps, 0.0)), 0.0)
    scores = jnp.einsum('thd,shd->hts', query_blk.astype(jnp.float32), key_blk.astype(jnp.float32))
    scaled_scores = (scores * mask_weights).astype(jnp.bfloat16)
    inside = jnp.einsum('hts,shd->thd', scaled_scores.astype(jnp.float32), value_blk.astype(jnp.float32))
    outside = jnp.einsum('thd,hde->the', query_blk.astype(jnp.float32), prior_state, precision=highest)
    outside = outside * jnp.exp(cumulative).T[:, :, None]
    attended = inside + outside
    normed = attended * lax.rsqrt(lax.optimization_barrier(jnp.mean(attended * attended, axis=2, keepdims=True)) + epsilon)
    block_total = cumulative[:, -1]
    keep_factor = jnp.exp(block_total[:, None] - cumulative)
    weighted_keys = key_blk.astype(jnp.float32) * keep_factor.T[:, :, None]
    block_state = jnp.einsum('thd,the->hde', weighted_keys, value_blk.astype(jnp.float32), precision=highest)
    next_state = jnp.exp(block_total)[:, None, None] * prior_state + block_state
    return (next_state, normed.astype(jnp.bfloat16))

def run_expert(bundle):
    rows_in, gate_w, up_w, down_w = bundle
    gate_proj = jnp.dot(rows_in, gate_w, preferred_element_type=jnp.float32)
    up_proj = jnp.dot(rows_in, up_w, preferred_element_type=jnp.float32)
    active = (jax.nn.silu(gate_proj) * up_proj).astype(jnp.bfloat16)
    group_width = FF // N_CTX

    def add_group(group, accumulated):
        offset = (group * group_width).astype(jnp.int32)
        columns = lax.dynamic_slice_in_dim(active, offset, group_width, 1)
        weight_rows = lax.dynamic_slice_in_dim(down_w, offset, group_width, 0)
        product = jnp.dot(columns, weight_rows, preferred_element_type=jnp.float32).astype(jnp.bfloat16)
        product = lax.optimization_barrier(product)
        return accumulated + product.astype(jnp.float32)
    initial = jnp.zeros((rows_in.shape[0], D), jnp.float32)
    summed = lax.fori_loop(0, N_CTX, add_group, initial)
    return summed.astype(jnp.bfloat16)

def reference(query_rows, key_rows, value_rows, log_decay, residual, out_weight, router_weight, expert_ids, expert_gate, expert_up, expert_down):
    tokens_all = query_rows.shape[0]
    blocks = tokens_all // TOK_DEV

    def to_heads(matrix):
        return matrix.reshape(blocks, TOK_DEV, HEAD_TOTAL, HEAD_SIZE)
    decay_blocks = log_decay.reshape(HEAD_TOTAL, blocks, TOK_DEV).transpose(1, 0, 2)
    initial = jnp.zeros((HEAD_TOTAL, HEAD_SIZE, HEAD_SIZE), jnp.float32)
    last_state, normed = lax.scan(attend_block, initial, (to_heads(query_rows), to_heads(key_rows), to_heads(value_rows), decay_blocks))
    normed = normed.reshape(tokens_all, HEAD_TOTAL * HEAD_SIZE)
    projected = jnp.dot(normed, out_weight, preferred_element_type=jnp.float32)
    hidden = (residual.astype(jnp.float32) + projected).astype(jnp.bfloat16)
    wide_rows = hidden.astype(jnp.float32)
    scaled = (wide_rows * lax.rsqrt(lax.optimization_barrier(jnp.mean(wide_rows * wide_rows, axis=1, keepdims=True)) + epsilon)).astype(jnp.bfloat16)
    logits = jnp.dot(scaled, router_weight, preferred_element_type=jnp.float32)
    expert_range = jnp.arange(EXPERTS, dtype=jnp.int32)
    choice_hot = (expert_ids[:, :, None] == expert_range[None, None, :]).astype(jnp.int32)
    picked = lax.optimization_barrier(jnp.sum(logits[:, None, :] * choice_hot.astype(jnp.float32), axis=2))
    first_weight = jax.nn.sigmoid(picked[:, 0] - picked[:, 1])
    second_weight = jax.nn.sigmoid(picked[:, 1] - picked[:, 0])
    counts = lax.optimization_barrier(jnp.sum(choice_hot, axis=1)).astype(jnp.int32).reshape(blocks, TOK_DEV, EXPERTS)
    before = (jnp.cumsum(counts, axis=1, dtype=jnp.int32) - counts).reshape(tokens_all, EXPERTS)
    slot_index = lax.optimization_barrier(jnp.sum(before[:, None, :] * choice_hot, axis=2)).astype(jnp.int32)
    block_of = jnp.arange(tokens_all, dtype=jnp.int32) // TOK_DEV
    row_index = (block_of[:, None] * CAP + slot_index).astype(jnp.int32)
    buffer = jnp.zeros((EXPERTS, blocks * CAP, D), jnp.bfloat16)
    buffer = buffer.at[expert_ids[:, 0], row_index[:, 0]].set(scaled)
    buffer = buffer.at[expert_ids[:, 1], row_index[:, 1]].set(scaled)
    outputs = lax.map(run_expert, (buffer, expert_gate, expert_up, expert_down))
    first_rows = outputs[expert_ids[:, 0], row_index[:, 0]].astype(jnp.float32)
    second_rows = outputs[expert_ids[:, 1], row_index[:, 1]].astype(jnp.float32)
    weighted_first = lax.optimization_barrier((first_weight[:, None] * first_rows).astype(jnp.bfloat16))
    weighted_second = lax.optimization_barrier((second_weight[:, None] * second_rows).astype(jnp.bfloat16))
    mixture = (weighted_first.astype(jnp.float32) + weighted_second.astype(jnp.float32)).astype(jnp.bfloat16)
    return (hidden, mixture)
```

```python
import jax
import jax.numpy as jnp
from jax import lax
from jax.experimental import pallas as pl
from jax.experimental.pallas import tpu as pltpu

from jax.sharding import PartitionSpec as P

MESH = pl.DeviceIdType.MESH
SIDE = 4


def grid_place():
    me = lax.axis_index("ctx")
    return me // SIDE, me % SIDE


def chunk_at(half, u, v):
    u, v = (u + SIDE) % SIDE, (v + SIDE) % SIDE
    return u * SIDE + v if half == 0 else v * SIDE + u


def expert_kernel(
    x_ref, gate_hbm, up_hbm, down_hbm, out_ref,
    rows, gate_w, up_w, down_w, gate_acc, up_acc, active,
    rel_out, rel_in, full_out, full_in,
    weight_sem, g_send, g_recv, r_send, r_recv,
):
    y, z = grid_place()
    half_rows, width = rows.shape[2], rows.shape[3]
    sub = half_rows // 2
    place = ((y, z), (z, y))
    groups = (0, -1, 1, 2)
    first, second = pl.ds(0, sub), pl.ds(sub, sub)

    def axis_device(half, axis, step):
        u, v = place[half]
        return chunk_at(half, u + step, v) if axis == 0 else chunk_at(half, u, v + step)

    weight_copies = [
        pltpu.make_async_copy(src, dst, weight_sem.at[i])
        for i, (src, dst) in enumerate(((gate_hbm, gate_w), (up_hbm, up_w), (down_hbm, down_w)))
    ]
    for copy in weight_copies:
        copy.start()

    barrier = pltpu.get_barrier_semaphore()
    for axis in (0, 1):
        for step in (1, -1):
            pl.semaphore_signal(
                barrier, inc=1, device_id={"ctx": axis_device(0, axis, step)}, device_id_type=MESH
            )
    for half in (0, 1):
        u, v = place[half]
        rows[half, chunk_at(half, u, v)] = x_ref[pl.ds(half * half_rows, half_rows), :]
    gate_acc[...] = jnp.zeros_like(gate_acc)
    up_acc[...] = jnp.zeros_like(up_acc)
    pl.semaphore_wait(barrier, 4)

    def ring(half, ring_set, kind, step):
        u, v = place[half]
        axis = 0 if ring_set == 0 else 1
        held = (0, 0, -1, 1)[kind] + step
        if axis == 0:
            ref = rows.at[half, chunk_at(half, u + held, v)]
        else:
            ref = rows.at[half, chunk_at(half, u + groups[ring_set - 1], v + held)]
        if kind >= 2:
            ref = ref.at[first if kind == 2 else second]
        k = (half * 5 + ring_set) * 4 + kind
        return pltpu.make_async_remote_copy(
            src_ref=ref, dst_ref=ref, send_sem=g_send.at[k], recv_sem=g_recv.at[k],
            device_id={"ctx": axis_device(half, axis, 1 if kind % 2 == 0 else -1)}, device_id_type=MESH,
        )

    def send(half, ring_set, kind):
        ring(half, ring_set, kind, 0).start()

    def arrive(half, ring_set, kind):
        ring(half, ring_set, kind, -1 if kind % 2 == 0 else 1).wait_recv()

    def multiply(half, group):
        u, v = place[half]

        @pl.loop(0, SIDE)
        def _(i):
            chunk = chunk_at(half, u + groups[group], i)
            part = rows[half, chunk]
            depth = pl.ds(pl.multiple_of(chunk * width, width), width)
            gate_acc[half] += jnp.dot(part, gate_w[depth, :], preferred_element_type=jnp.float32)
            up_acc[half] += jnp.dot(part, up_w[depth, :], preferred_element_type=jnp.float32)

    both = (0, 1)
    for half in both:
        send(half, 0, 0)
        send(half, 0, 1)
    for half in both:
        send(half, 1, 0)
        send(half, 1, 1)
    for half in both:
        arrive(half, 0, 0)
        send(half, 0, 2)
        arrive(half, 0, 1)
        send(half, 0, 3)
    for group in (1, 2):
        for half in both:
            send(half, group + 1, 0)
            send(half, group + 1, 1)

    def relay(group):
        for half in both:
            arrive(half, group + 1, 0)
            send(half, group + 1, 2)
            arrive(half, group + 1, 1)
            send(half, group + 1, 3)

    def finish(group):
        for half in both:
            arrive(half, group + 1, 2)
            arrive(half, group + 1, 3)
            multiply(half, group)

    for half in both:
        arrive(half, 0, 2)
        arrive(half, 0, 3)
        send(half, 4, 0)
        send(half, 4, 1)
    relay(0)
    weight_copies[0].wait()
    weight_copies[1].wait()
    relay(1)
    finish(0)
    relay(2)
    finish(1)
    relay(3)
    finish(2)
    for half in both:
        arrive(half, 4, 2)
        arrive(half, 4, 3)
        multiply(half, 3)
        gate = gate_acc[half]
        active[half] = (gate * (1.0 / (1.0 + jnp.exp(-gate))) * up_acc[half]).astype(active.dtype)
    weight_copies[2].wait()

    order = (2, 1, -1, 0)

    def product(half, du, dv):
        u, v = place[half]
        chunk = chunk_at(half, u + dv, v + du)
        columns = pl.ds(pl.multiple_of(chunk * width, width), width)
        return jnp.dot(active[half], down_w[:, columns], preferred_element_type=jnp.float32)

    def reduce_copy(half, group, kind):
        axis = 1 if group < 4 else 0
        if kind < 2:
            part = first if kind == 0 else second
            src, dst = rel_out.at[half, group, part], rel_in.at[half, group, part]
        else:
            src, dst = full_out.at[half, group, kind - 2], full_in.at[half, group, kind - 2]
        k = (half * 5 + group) * 4 + kind
        return pltpu.make_async_remote_copy(
            src_ref=src, dst_ref=dst, send_sem=r_send.at[k], recv_sem=r_recv.at[k],
            device_id={"ctx": axis_device(half, axis, 1 if kind % 2 == 0 else -1)}, device_id_type=MESH,
        )

    def far(half, group, value):
        rel_out[half, group] = value.astype(rel_out.dtype)
        reduce_copy(half, group, 0).start()
        reduce_copy(half, group, 1).start()

    def near(half, group, way, value):
        full_out[half, group, way] = value.astype(full_out.dtype)
        part = first if way == 0 else second
        start = way * sub
        reduce_copy(half, group, way).wait_recv()
        full_out[half, group, way, part] = (
            value[start:start + sub] + rel_in[half, group, part].astype(jnp.float32)
        ).astype(full_out.dtype)
        reduce_copy(half, group, 2 + way).start()

    def total(half, group, value):
        for way in (0, 1):
            reduce_copy(half, group, 2 + way).wait_recv()
            value = value + full_in[half, group, way].astype(jnp.float32)
        return value

    for group in range(4):
        for half in both:
            far(half, group, product(half, 2, order[group]))
    for group in range(4):
        for half in both:
            near(half, group, 0, product(half, 1, order[group]))
            near(half, group, 1, product(half, -1, order[group]))
    for group in range(4):
        for half in both:
            value = total(half, group, product(half, 0, order[group]))
            if group == 0:
                far(half, 4, value)
            elif group < 3:
                near(half, 4, group - 1, value)
            else:
                value = total(half, 4, value)
                out_ref[pl.ds(half * half_rows, half_rows), :] = value.astype(out_ref.dtype)

    for half in both:
        for ring_set in range(5):
            for kind in range(4):
                ring(half, ring_set, kind, 0).wait_send()
                reduce_copy(half, ring_set, kind).wait_send()


def run_experts(x, gate_w, up_w, down_w):
    slots, width = x.shape
    half_rows = slots // 2
    model, units = gate_w.shape
    blocks = (2, 5, half_rows, width)
    kind = x.dtype
    return pl.pallas_call(
        expert_kernel,
        out_shape=jax.ShapeDtypeStruct((slots, width), kind),
        in_specs=[pl.BlockSpec(memory_space=pltpu.VMEM)] + [pl.BlockSpec(memory_space=pl.ANY)] * 3,
        out_specs=pl.BlockSpec(memory_space=pltpu.VMEM),
        scratch_shapes=[
            pltpu.VMEM((2, SIDE * SIDE, half_rows, width), kind),
            pltpu.VMEM((model, units), kind),
            pltpu.VMEM((model, units), kind),
            pltpu.VMEM((units, model), kind),
            pltpu.VMEM((2, half_rows, units), jnp.float32),
            pltpu.VMEM((2, half_rows, units), jnp.float32),
            pltpu.VMEM((2, half_rows, units), kind),
            pltpu.VMEM(blocks, kind),
            pltpu.VMEM(blocks, kind),
            pltpu.VMEM((2, 5, 2, half_rows, width), kind),
            pltpu.VMEM((2, 5, 2, half_rows, width), kind),
            pltpu.SemaphoreType.DMA((3,)),
            pltpu.SemaphoreType.DMA((40,)),
            pltpu.SemaphoreType.DMA((40,)),
            pltpu.SemaphoreType.DMA((40,)),
            pltpu.SemaphoreType.DMA((40,)),
        ],
        compiler_params=pltpu.CompilerParams(
            collective_id=1, has_side_effects=True, vmem_limit_bytes=60 * 1024 * 1024
        ),
        cost_estimate=pl.CostEstimate(
            flops=6 * slots * model * units, bytes_accessed=6 * model * units, transcendentals=0
        ),
    )(x, gate_w, up_w, down_w)


epsilon = 1e-05
highest = lax.Precision.HIGHEST


def carried_in(array, axis, combine, identity):
    size, index = (lax.axis_size(axis), lax.axis_index(axis))
    everything = jax.tree.map(
        lambda part, kind: lax.all_gather(part.astype(kind), axis),
        array,
        (jnp.bfloat16, jnp.bfloat16),
    )
    start = jax.tree.map(
        lambda part, zero: jnp.broadcast_to(jnp.asarray(zero, part.dtype), part.shape),
        array,
        identity,
    )

    def step(k, before):
        reached = k < index
        new = combine(
            before, jax.tree.map(lambda part, own: part[k].astype(own.dtype), everything, array)
        )
        return jax.tree.map(lambda a, b: jnp.where(reached, a, b), new, before)

    return lax.fori_loop(0, size, step, start)


def per_device(
    query_rows,
    key_rows,
    value_rows,
    log_decay,
    residual,
    out_weight,
    router_weight,
    expert_ids,
    expert_gate,
    expert_up,
    expert_down,
):
    length = query_rows.shape[0]
    head_count = log_decay.shape[0]
    head_width = query_rows.shape[1] // head_count
    query_heads = query_rows.reshape(length, head_count, head_width)
    key_heads = key_rows.reshape(length, head_count, head_width)
    value_heads = value_rows.reshape(length, head_count, head_width)
    cumulative = jnp.cumsum(log_decay, axis=1)
    row_index = lax.broadcasted_iota(jnp.int32, (length, length), 0)
    col_index = lax.broadcasted_iota(jnp.int32, (length, length), 1)
    gaps = cumulative[:, :, None] - cumulative[:, None, :]
    mask_weights = jnp.where((col_index <= row_index)[None], jnp.exp(jnp.minimum(gaps, 0.0)), 0.0)
    scores = jnp.einsum("thd,shd->hts", query_heads, key_heads, preferred_element_type=jnp.float32)
    scaled_scores = (scores * mask_weights).astype(jnp.bfloat16)
    inside = jnp.einsum(
        "hts,shd->thd", scaled_scores, value_heads, preferred_element_type=jnp.float32
    )
    block_total = cumulative[:, -1]
    keep_factor = jnp.exp(block_total[:, None] - cumulative)
    weighted_keys = key_heads.astype(jnp.float32) * keep_factor.T[:, :, None]
    block_state = jnp.einsum(
        "thd,the->hde", weighted_keys, value_heads.astype(jnp.float32), precision=highest
    )

    def combine_pair(earlier_pair, later_pair):
        merged_total = earlier_pair[0] + later_pair[0]
        merged_state = jnp.exp(later_pair[0])[:, None, None] * earlier_pair[1] + later_pair[1]
        return (merged_total, merged_state)

    empty_pair = (jnp.zeros_like(block_total), jnp.zeros_like(block_state))
    prior_total, prior_state = carried_in(
        (block_total, block_state), "ctx", combine_pair, empty_pair
    )
    outside = jnp.einsum(
        "thd,hde->the", query_heads.astype(jnp.float32), prior_state, precision=highest
    )
    outside = outside * jnp.exp(cumulative).T[:, :, None]
    attended = inside + outside
    normed = attended * lax.rsqrt(jnp.mean(attended * attended, axis=2, keepdims=True) + epsilon)
    normed = normed.astype(jnp.bfloat16).reshape(length, head_count * head_width)
    partial_value = jnp.dot(
        normed,
        lax.all_gather(out_weight, "ctx", axis=1, tiled=True),
        preferred_element_type=jnp.float32,
    )
    projected = lax.psum_scatter(
        partial_value.astype(jnp.bfloat16), "exp", scatter_dimension=1, tiled=True
    ).astype(jnp.float32)
    hidden = (residual.astype(jnp.float32) + projected).astype(jnp.bfloat16)
    whole = lax.all_gather(hidden, "exp", axis=1, tiled=True)
    wide_rows = whole.astype(jnp.float32)
    scaled = (
        wide_rows * lax.rsqrt(jnp.mean(wide_rows * wide_rows, axis=1, keepdims=True) + epsilon)
    ).astype(jnp.bfloat16)
    logits = jnp.dot(scaled, router_weight, preferred_element_type=jnp.float32)
    expert_count = router_weight.shape[1]
    expert_range = jnp.arange(expert_count, dtype=jnp.int32)
    choice_hot = (expert_ids[:, :, None] == expert_range[None, None, :]).astype(jnp.int32)
    picked = jnp.sum(logits[:, None, :] * choice_hot.astype(jnp.float32), axis=2)
    first_weight = jax.nn.sigmoid(picked[:, 0] - picked[:, 1])
    second_weight = jax.nn.sigmoid(picked[:, 1] - picked[:, 0])
    token_weight = first_weight[:, None] * choice_hot[:, 0, :].astype(jnp.float32) + second_weight[
        :, None
    ] * choice_hot[:, 1, :].astype(jnp.float32)
    counts = jnp.sum(choice_hot, axis=1)
    before = jnp.cumsum(counts, axis=0, dtype=jnp.int32) - counts
    slot_index = jnp.sum(before[:, None, :] * choice_hot, axis=2)
    capacity = 2 * length // lax.axis_size("exp") + length // 32
    slot_hot = (
        slot_index[:, :, None] == jnp.arange(capacity, dtype=jnp.int32)[None, None, :]
    ).astype(jnp.bfloat16)
    dispatch = jnp.einsum(
        "tje,tjc->etc",
        choice_hot.astype(jnp.bfloat16),
        slot_hot,
        preferred_element_type=jnp.float32,
    ).astype(jnp.bfloat16)
    own_expert = lax.axis_index("exp")
    own_dispatch = lax.dynamic_index_in_dim(dispatch, own_expert, 0, keepdims=False)
    slot_input = jnp.einsum(
        "tc,td->cd", own_dispatch, scaled, preferred_element_type=jnp.float32
    ).astype(jnp.bfloat16)
    gate_w = expert_gate[0]
    up_w = expert_up[0]
    down_w = expert_down[0]
    chunk_rows = lax.all_to_all(slot_input, "ctx", split_axis=1, concat_axis=0, tiled=True)
    chunk_out = run_experts(chunk_rows, gate_w, up_w, down_w)
    expert_out = lax.all_to_all(chunk_out, "ctx", split_axis=0, concat_axis=1, tiled=True)
    own_weight = lax.dynamic_index_in_dim(token_weight, own_expert, 1, keepdims=False)
    returned = jnp.dot(own_dispatch, expert_out, preferred_element_type=jnp.float32)
    weighted = lax.optimization_barrier((own_weight[:, None] * returned).astype(jnp.bfloat16))
    summed = lax.psum_scatter(
        weighted.astype(jnp.float32).astype(jnp.bfloat16), "exp", scatter_dimension=1, tiled=True
    )
    return (hidden, summed)


def solution(mesh):
    return jax.shard_map(
        per_device,
        mesh=mesh,
        in_specs=(
            P("ctx", "exp"),
            P("ctx", "exp"),
            P("ctx", "exp"),
            P("exp", "ctx"),
            P("ctx", "exp"),
            P("exp", "ctx"),
            P(),
            P("ctx", None),
            P("exp", None, "ctx"),
            P("exp", None, "ctx"),
            P("exp", "ctx", None),
        ),
        out_specs=(P("ctx", "exp"), P("ctx", "exp")),
        check_vma=False,
    )
```

```python
import jax
import jax.numpy as jnp
from jax import lax
from jax.experimental import pallas as pl
from jax.experimental.pallas import tpu as pltpu
from jax.sharding import PartitionSpec as P

MESH = pl.DeviceIdType.MESH
SIDE = 4
CTX = 16
EXP = 8
PAD = 80
GROUPS = (0, -1, 1, 2)
FAR_FIRST = (2, 1, -1, 0)
BOTH = (0, 1)
epsilon = 1e-05
highest = lax.Precision.HIGHEST


def dot(a, b):
    return jnp.dot(a, b, preferred_element_type=jnp.float32)


def dot_rows(a, b):
    return lax.dot_general(a, b, (((1,), (1,)), ((), ())), preferred_element_type=jnp.float32)


def chunk_at(half, u, v):
    u, v = (u + SIDE) % SIDE, (v + SIDE) % SIDE
    return u * SIDE + v if half == 0 else v * SIDE + u


def plane_device(half, axis, step):
    me = lax.axis_index("ctx")
    y, z = me // SIDE, me % SIDE
    u, v = (y, z) if half == 0 else (z, y)
    return chunk_at(half, u + step, v) if axis == 0 else chunk_at(half, u, v + step)


class Gather:
    def __init__(self, buf, send_sem, recv_sem):
        self.buf, self.send_sem, self.recv_sem = buf, send_sem, recv_sem
        self.half_rows = buf.shape[1] // 2
        me = lax.axis_index("ctx")
        y, z = me // SIDE, me % SIDE
        self.place = ((y, z), (z, y))

    def copy(self, half, ring, kind, step):
        u, v = self.place[half]
        axis = 0 if ring == 0 else 1
        held = (0, 0, -1, 1)[kind] + step
        if axis == 0:
            chunk = chunk_at(half, u + held, v)
        else:
            chunk = chunk_at(half, u + GROUPS[ring - 1], v + held)
        start, size = half * self.half_rows, self.half_rows
        if kind >= 2:
            size = size // 2
            start = start + (kind - 2) * size
        ref = self.buf.at[chunk, pl.ds(start, size)]
        k = (half * 5 + ring) * 4 + kind
        return pltpu.make_async_remote_copy(
            src_ref=ref,
            dst_ref=ref,
            send_sem=self.send_sem.at[k],
            recv_sem=self.recv_sem.at[k],
            device_id={"ctx": plane_device(half, axis, 1 if kind % 2 == 0 else -1)},
            device_id_type=MESH,
        )

    def send(self, half, ring, kind):
        self.copy(half, ring, kind, 0).start()

    def arrive(self, half, ring, kind):
        self.copy(half, ring, kind, -1 if kind % 2 == 0 else 1).wait_recv()

    def begin(self):
        for half in BOTH:
            self.send(half, 0, 0)
            self.send(half, 0, 1)
        for half in BOTH:
            self.send(half, 1, 0)
            self.send(half, 1, 1)

    def first_axis(self):
        for half in BOTH:
            self.arrive(half, 0, 0)
            self.send(half, 0, 2)
            self.arrive(half, 0, 1)
            self.send(half, 0, 3)
        for ring in (2, 3):
            for half in BOTH:
                self.send(half, ring, 0)
                self.send(half, ring, 1)
        for half in BOTH:
            self.arrive(half, 0, 2)
            self.arrive(half, 0, 3)
            self.send(half, 4, 0)
            self.send(half, 4, 1)

    def relay(self, group):
        for half in BOTH:
            self.arrive(half, group + 1, 0)
            self.send(half, group + 1, 2)
            self.arrive(half, group + 1, 1)
            self.send(half, group + 1, 3)

    def settle(self, half, group):
        self.arrive(half, group + 1, 2)
        self.arrive(half, group + 1, 3)

    def drain(self):
        for half in BOTH:
            for ring in range(5):
                for kind in range(4):
                    self.copy(half, ring, kind, 0).wait_send()


class RingSum:
    def __init__(self, rel_out, rel_in, full_out, full_in, send_sem, recv_sem, base, device):
        self.refs = (rel_out, rel_in, full_out, full_in)
        self.send_sem, self.recv_sem, self.base, self.device = send_sem, recv_sem, base, device
        self.sub = rel_out.shape[0] // 2

    def copy(self, kind):
        rel_out, rel_in, full_out, full_in = self.refs
        if kind < 2:
            part = pl.ds(kind * self.sub, self.sub)
            src, dst = rel_out.at[part], rel_in.at[part]
        else:
            src, dst = full_out.at[kind - 2], full_in.at[kind - 2]
        return pltpu.make_async_remote_copy(
            src_ref=src,
            dst_ref=dst,
            send_sem=self.send_sem.at[self.base + kind],
            recv_sem=self.recv_sem.at[self.base + kind],
            device_id=self.device(1 if kind % 2 == 0 else -1),
            device_id_type=MESH,
        )

    def far(self, value):
        rel_out = self.refs[0]
        rel_out[...] = value.astype(rel_out.dtype)
        self.copy(0).start()
        self.copy(1).start()

    def near(self, way, value):
        _, rel_in, full_out, _ = self.refs
        full_out[way] = value.astype(full_out.dtype)
        start = way * self.sub
        part = pl.ds(start, self.sub)
        self.copy(way).wait_recv()
        full_out[way, part] = (
            value[start : start + self.sub] + rel_in[part].astype(jnp.float32)
        ).astype(full_out.dtype)
        self.copy(2 + way).start()

    def total(self, value):
        full_in = self.refs[3]
        for way in BOTH:
            self.copy(2 + way).wait_recv()
            value = value + full_in[way].astype(jnp.float32)
        return value

    def drain(self):
        for kind in range(4):
            self.copy(kind).wait_send()


def layer_kernel(
    normed_ref, residual_ref, out_w, router_ref, ids_ref, gate_hbm, up_hbm, down_hbm,
    hidden_ref, mixture_ref,
    normed_all, pair_out, pair_in, proj_rel_out, proj_rel_in, proj_full_out, proj_full_in,
    res_out, res_in, ids_out, ids_in, hid_out, hid_in, mix_out, mix_in,
    picks, disp_out, disp_in, stat_out, stat_in, scale_out, scale_in, scale_col, token_weight,
    rows, gate_w, up_w, down_w, gate_acc, up_acc, active,
    rel_out, rel_in, full_out, full_in, ret_out, ret_in,
    weight_sem, n_send, n_recv, g_send, g_recv, r_send, r_recv, p_send, p_recv, q_send, q_recv,
    swap_send, swap_recv, d_send, d_recv, s_send, s_recv, c_send, c_recv, b_send, b_recv,
):
    ctx, exp = lax.axis_index("ctx"), lax.axis_index("exp")
    y, z = ctx // SIDE, ctx % SIDE
    x, core = exp // 2, exp % 2
    length, part_width = res_in.shape[1], res_in.shape[2]
    width = rows.shape[2]
    slots = rows.shape[1]
    pair_slots = slots // EXP
    half_rows = slots // 2
    model = down_w.shape[1]
    f32, kind = jnp.float32, rows.dtype
    place = ((y, z), (z, y))

    weight_copies = [
        pltpu.make_async_copy(src, dst, weight_sem.at[i])
        for i, (src, dst) in enumerate(((gate_hbm, gate_w), (up_hbm, up_w), (down_hbm, down_w)))
    ]
    for copy in weight_copies:
        copy.start()

    def partner(i):
        return {"ctx": 2 * exp + i, "exp": ctx // 2}

    def partner_is_me(i):
        return jnp.logical_and(ctx == 2 * exp + i, exp == ctx // 2)

    slot = ctx % 2
    barrier = pltpu.get_barrier_semaphore()

    @pl.loop(1, CTX)
    def _(k):
        pl.semaphore_signal(barrier, inc=1, device_id={"ctx": (ctx + k) % CTX}, device_id_type=MESH)

    @pl.loop(1, EXP)
    def _(k):
        pl.semaphore_signal(barrier, inc=1, device_id={"exp": (exp + k) % EXP}, device_id_type=MESH)

    for i in BOTH:

        @pl.when(jnp.logical_not(partner_is_me(i)))
        def _():
            pl.semaphore_signal(barrier, inc=1, device_id=partner(i), device_id_type=MESH)

    normed_all[ctx] = normed_ref[...]
    ids_out[0:2, :] = ids_ref[...]
    for i in BOTH:
        res_out[i] = residual_ref[:, i * part_width : (i + 1) * part_width]
    gate_acc[...] = jnp.zeros_like(gate_acc)
    up_acc[...] = jnp.zeros_like(up_acc)
    pl.semaphore_wait(barrier, CTX + EXP - 2 + jnp.where(exp == ctx // 2, 1, 2))

    def swap(index, i, src, dst, mine):
        def copy(arriving):
            k = 2 * index
            return pltpu.make_async_remote_copy(
                src_ref=src,
                dst_ref=dst.at[i] if arriving else dst.at[slot],
                send_sem=swap_send.at[k + i],
                recv_sem=swap_recv.at[k + i] if arriving else swap_recv.at[k + slot],
                device_id=partner(i),
                device_id_type=MESH,
            )

        def start():
            @pl.when(partner_is_me(i))
            def _():
                mine()

            @pl.when(jnp.logical_not(partner_is_me(i)))
            def _():
                copy(False).start()

        def arrive():
            @pl.when(jnp.logical_not(partner_is_me(i)))
            def _():
                copy(True).wait_recv()

        def drain():
            @pl.when(jnp.logical_not(partner_is_me(i)))
            def _():
                copy(False).wait_send()

        return start, arrive, drain

    def keep(src, i, dst):
        def mine():
            dst[i] = src[i]

        return mine

    def keep_ids(i):
        def mine():
            ids_in[i] = ids_out[...]

        return mine

    gather = Gather(normed_all, n_send, n_recv)
    gather.begin()
    swaps_res = [swap(0, i, res_out.at[i], res_in, keep(res_out, i, res_in)) for i in BOTH]
    swaps_ids = [swap(1, i, ids_out, ids_in, keep_ids(i)) for i in BOTH]
    for start, _, _ in swaps_res + swaps_ids:
        start()
    gather.first_axis()
    gather.relay(0)
    gather.relay(1)
    for half in BOTH:
        gather.settle(half, 0)
    gather.relay(2)
    for half in BOTH:
        gather.settle(half, 1)
    gather.relay(3)
    for _, arrive, _ in swaps_ids:
        arrive()

    expert_row = lax.broadcasted_iota(jnp.int32, (EXP, length), 0)
    later = (
        lax.broadcasted_iota(jnp.int32, (length, length), 0)
        < lax.broadcasted_iota(jnp.int32, (length, length), 1)
    ).astype(jnp.bfloat16)
    named = []
    for i in BOTH:
        chosen = [expert_row == ids_in[i, k : k + 1, :] for k in BOTH]
        count = chosen[0].astype(f32) + chosen[1].astype(f32)
        before = dot(count.astype(jnp.bfloat16), later)
        key = jnp.where(count > 0.5, before + float(i * (pair_slots // 2)), -1.0)
        named.append((key, chosen))
    key = jnp.concatenate([named[0][0], named[1][0]], axis=1)
    slot_row = lax.broadcasted_iota(jnp.int32, (128, 2 * length), 0).astype(f32)
    for e in range(EXP):
        picks[e] = jnp.where(slot_row == key[e : e + 1, :], 1.0, 0.0).astype(picks.dtype)

    for group in (2, 3):
        for half in BOTH:
            gather.settle(half, group)

    def project(x_to, core_to):
        blocks = normed_all[pl.ds(2 * (x_to * 2 + core_to), 2)]
        return dot(blocks.reshape(2 * length, blocks.shape[2]), out_w[...])

    def pair_copy(i):
        return pltpu.make_async_remote_copy(
            src_ref=pair_out.at[i],
            dst_ref=pair_in.at[i],
            send_sem=p_send.at[i],
            recv_sem=p_recv.at[i],
            device_id={"exp": x * 2 + 1 - core},
            device_id_type=MESH,
        )

    for i, step in enumerate(FAR_FIRST):
        pair_out[i] = project((x + step + SIDE) % SIDE, 1 - core).astype(kind)
        pair_copy(i).start()
    proj_sum = RingSum(
        proj_rel_out, proj_rel_in, proj_full_out, proj_full_in, q_send, q_recv, 0,
        lambda step: {"exp": ((x + step + SIDE) % SIDE) * 2 + core},
    )
    for i, step in enumerate(FAR_FIRST):
        value = project((x + step + SIDE) % SIDE, core)
        pair_copy(i).wait_recv()
        value = value + pair_in[i].astype(f32)
        if i == 0:
            proj_sum.far(value)
        elif i < 3:
            proj_sum.near(i - 1, value)
        else:
            value = proj_sum.total(value)
    for _, arrive, _ in swaps_res:
        arrive()
    hid = (res_in[...].reshape(2 * length, part_width).astype(f32) + value).astype(kind)
    hid_out[...] = hid.reshape(2, length, part_width)

    def disp_copy(k, src_exp):
        return pltpu.make_async_remote_copy(
            src_ref=disp_out.at[(exp + k) % EXP],
            dst_ref=disp_in.at[src_exp],
            send_sem=d_send.at[k],
            recv_sem=d_recv.at[k],
            device_id={"exp": (exp + k) % EXP},
            device_id_type=MESH,
        )

    @pl.loop(1, EXP)
    def _(k):
        to = (exp + k) % EXP
        disp_out[to] = dot(picks[to, pl.ds(0, PAD), :], hid).astype(kind)
        disp_copy(k, exp).start()

    disp_in[exp] = dot(picks[exp, pl.ds(0, PAD), :], hid).astype(kind)

    swaps_hid = [swap(2, i, hid_out.at[i], hid_in, keep(hid_out, i, hid_in)) for i in BOTH]
    for start, _, _ in swaps_hid:
        start()

    wide = hid.astype(f32)
    columns = pl.ds(pl.multiple_of(ctx * width, width), width)
    stat_out[pl.ds(0, EXP), :] = dot_rows(router_ref[:, columns], hid)
    stat_out[pl.ds(EXP, EXP), :] = lax.dot_general(
        jnp.ones((EXP, width), f32), wide * wide, (((1,), (1,)), ((), ())),
        preferred_element_type=f32, precision=highest,
    )
    stat_in[ctx] = stat_out[...]

    def stat_copy(k, src_ctx):
        return pltpu.make_async_remote_copy(
            src_ref=stat_out,
            dst_ref=stat_in.at[src_ctx],
            send_sem=s_send.at[k],
            recv_sem=s_recv.at[k],
            device_id={"ctx": (ctx + k) % CTX},
            device_id_type=MESH,
        )

    @pl.loop(1, CTX)
    def _(k):
        stat_copy(k, ctx).start()

    @pl.loop(1, EXP)
    def _(k):
        disp_copy(k, (exp + EXP - k) % EXP).wait_recv()

    rows[ctx] = (
        disp_in[...].astype(f32)[:, :pair_slots, :].reshape(slots, width).astype(kind)
    )

    def multiply(half, group):
        u, v = place[half]
        part_rows = pl.ds(half * half_rows, half_rows)

        @pl.loop(0, SIDE)
        def _(i):
            chunk = chunk_at(half, u + GROUPS[group], i)
            part = rows[chunk, part_rows, :]
            depth = pl.ds(pl.multiple_of(chunk * width, width), width)
            gate_acc[half] += dot_rows(part, gate_w[:, depth])
            up_acc[half] += dot_rows(part, up_w[:, depth])

    spread = Gather(rows, g_send, g_recv)
    spread.begin()
    spread.first_axis()
    spread.relay(0)

    @pl.loop(1, CTX)
    def _(k):
        stat_copy(k, (ctx + CTX - k) % CTX).wait_recv()

    stats = stat_in[0]
    for k in range(1, CTX):
        stats = stats + stat_in[k]
    row_scale = lax.rsqrt(stats[EXP:, :] * (1.0 / model) + epsilon)
    logits = stats[:EXP, :] * row_scale
    high = row_scale.astype(jnp.bfloat16).astype(f32)
    middle = (row_scale - high).astype(jnp.bfloat16).astype(f32)
    low = row_scale - high - middle
    which = lax.broadcasted_iota(jnp.int32, row_scale.shape, 0)
    thirds = jnp.where(
        which == 0, high, jnp.where(which == 1, middle, jnp.where(which == 2, low, 0.0))
    ).astype(jnp.bfloat16)

    def scale_copy(k, src_exp):
        return pltpu.make_async_remote_copy(
            src_ref=scale_out.at[(exp + k) % EXP],
            dst_ref=scale_in.at[src_exp],
            send_sem=c_send.at[k],
            recv_sem=c_recv.at[k],
            device_id={"exp": (exp + k) % EXP},
            device_id_type=MESH,
        )

    @pl.loop(1, EXP)
    def _(k):
        to = (exp + k) % EXP
        scale_out[to] = dot_rows(thirds, picks[to])
        scale_copy(k, exp).start()

    scale_in[exp] = dot_rows(thirds, picks[exp])

    picked = []
    for k in BOTH:
        chosen = jnp.concatenate([named[0][1][k], named[1][1][k]], axis=1)
        picked.append(jnp.sum(jnp.where(chosen, logits, 0.0), axis=0, keepdims=True))
    first_weight = 1.0 / (1.0 + jnp.exp(picked[1] - picked[0]))
    second_weight = 1.0 / (1.0 + jnp.exp(picked[0] - picked[1]))
    token_weight[...] = jnp.where(
        which == 0, first_weight, jnp.where(which == 1, second_weight, 0.0)
    ).T

    weight_copies[0].wait()
    weight_copies[1].wait()
    spread.relay(1)
    for half in BOTH:
        spread.settle(half, 0)
        multiply(half, 0)
    spread.relay(2)
    for half in BOTH:
        spread.settle(half, 1)
        multiply(half, 1)
    spread.relay(3)

    @pl.loop(1, EXP)
    def _(k):
        scale_copy(k, (exp + EXP - k) % EXP).wait_recv()

    row_scales = jnp.sum(scale_in[...], axis=1).T
    for e in range(EXP):
        scale_col[pl.ds(e * pair_slots, pair_slots), :] = jnp.broadcast_to(
            row_scales[:pair_slots, e : e + 1], (pair_slots, 128)
        )
    for half in BOTH:
        spread.settle(half, 2)
        multiply(half, 2)
    for half in BOTH:
        spread.settle(half, 3)
        multiply(half, 3)
        scale = scale_col[pl.ds(half * half_rows, half_rows), 0:1]
        gate = gate_acc[half] * scale
        up = up_acc[half] * scale
        active[half] = (gate * (1.0 / (1.0 + jnp.exp(-gate))) * up).astype(kind)
    weight_copies[2].wait()

    def product(half, du, dv):
        u, v = place[half]
        chunk = chunk_at(half, u + dv, v + du)
        return dot(active[half], down_w[:, pl.ds(pl.multiple_of(chunk * width, width), width)])

    def ring_device(half, axis):
        return lambda step: {"ctx": plane_device(half, axis, step)}

    sums = [
        [
            RingSum(
                rel_out.at[half, group], rel_in.at[half, group],
                full_out.at[half, group], full_in.at[half, group],
                r_send, r_recv, (half * 5 + group) * 4, ring_device(half, 1 if group < 4 else 0),
            )
            for group in range(5)
        ]
        for half in BOTH
    ]

    def back_copy(k, src_exp):
        return pltpu.make_async_remote_copy(
            src_ref=ret_out.at[(exp + k) % EXP],
            dst_ref=ret_in.at[src_exp],
            send_sem=b_send.at[k],
            recv_sem=b_recv.at[k],
            device_id={"exp": (exp + k) % EXP},
            device_id_type=MESH,
        )

    for group in range(4):
        for half in BOTH:
            sums[half][group].far(product(half, 2, FAR_FIRST[group]))
    for group in range(4):
        for half in BOTH:
            sums[half][group].near(0, product(half, 1, FAR_FIRST[group]))
            sums[half][group].near(1, product(half, -1, FAR_FIRST[group]))
    blank = jnp.zeros((PAD - pair_slots, width), f32)
    for group in range(4):
        for half in BOTH:
            value = sums[half][group].total(product(half, 0, FAR_FIRST[group]))
            if group == 0:
                sums[half][4].far(value)
            elif group < 3:
                sums[half][4].near(group - 1, value)
            else:
                value = sums[half][4].total(value)
                for i in range(EXP // 2):
                    part = value[i * pair_slots : (i + 1) * pair_slots]
                    ret_out[half * (EXP // 2) + i] = jnp.concatenate([part, blank], axis=0).astype(kind)

    @pl.loop(1, EXP)
    def _(k):
        back_copy(k, exp).start()

    ret_in[exp] = ret_out[exp]

    @pl.loop(1, EXP)
    def _(k):
        back_copy(k, (exp + EXP - k) % EXP).wait_recv()

    back = ret_in[...].reshape(EXP * PAD, width)
    weighted = []
    for k in BOTH:
        chosen = jnp.concatenate([named[0][1][k], named[1][1][k]], axis=1)
        take = jnp.concatenate(
            [
                jnp.where(chosen[e : e + 1, :], picks[e, pl.ds(0, PAD), :].astype(f32), 0.0)
                for e in range(EXP)
            ],
            axis=0,
        ).T.astype(kind)
        weighted.append((dot(take, back) * token_weight[:, k : k + 1]).astype(kind).astype(f32))
    mix_out[...] = (weighted[0] + weighted[1]).astype(kind).reshape(2, length, part_width)
    swaps_mix = [swap(3, i, mix_out.at[i], mix_in, keep(mix_out, i, mix_in)) for i in BOTH]
    for start, _, _ in swaps_mix:
        start()
    for _, arrive, _ in swaps_hid + swaps_mix:
        arrive()
    for i in BOTH:
        hidden_ref[:, i * part_width : (i + 1) * part_width] = hid_in[i]
        mixture_ref[:, i * part_width : (i + 1) * part_width] = mix_in[i]

    gather.drain()
    spread.drain()
    proj_sum.drain()
    for i in range(4):
        pair_copy(i).wait_send()
    for half in BOTH:
        for group in range(5):
            sums[half][group].drain()
    for _, _, drain in swaps_res + swaps_ids + swaps_hid + swaps_mix:
        drain()

    @pl.loop(1, EXP)
    def _(k):
        disp_copy(k, exp).wait_send()
        scale_copy(k, exp).wait_send()
        back_copy(k, exp).wait_send()

    @pl.loop(1, CTX)
    def _(k):
        stat_copy(k, ctx).wait_send()


def project_and_mix(normed, residual, out_weight, router, ids, gate_w, up_w, down_w):
    length, inner = normed.shape
    width = out_weight.shape[1]
    units, model = down_w.shape
    slots = CTX * (2 * length // EXP + length // 32)
    half_rows = slots // 2
    kind, f32 = normed.dtype, jnp.float32
    vmem = pl.BlockSpec(memory_space=pltpu.VMEM)
    anywhere = pl.BlockSpec(memory_space=pl.ANY)
    two = (2, length, width)
    dma = pltpu.SemaphoreType.DMA
    out = jax.ShapeDtypeStruct(residual.shape, kind)
    blocks = (2, 5, half_rows, width)
    return pl.pallas_call(
        layer_kernel,
        out_shape=(out, out),
        in_specs=[vmem] * 5 + [anywhere] * 3,
        out_specs=(vmem, vmem),
        scratch_shapes=[
            pltpu.VMEM((CTX, length, inner), kind),
            pltpu.VMEM((4, 2 * length, width), kind),
            pltpu.VMEM((4, 2 * length, width), kind),
            pltpu.VMEM((2 * length, width), kind),
            pltpu.VMEM((2 * length, width), kind),
            pltpu.VMEM((2, 2 * length, width), kind),
            pltpu.VMEM((2, 2 * length, width), kind),
            pltpu.VMEM(two, kind),
            pltpu.VMEM(two, kind),
            pltpu.VMEM((8, length), jnp.int32),
            pltpu.VMEM((2, 8, length), jnp.int32),
            pltpu.VMEM(two, kind),
            pltpu.VMEM(two, kind),
            pltpu.VMEM(two, kind),
            pltpu.VMEM(two, kind),
            pltpu.VMEM((EXP, 128, 2 * length), kind),
            pltpu.VMEM((EXP, PAD, width), kind),
            pltpu.VMEM((EXP, PAD, width), kind),
            pltpu.VMEM((2 * EXP, 2 * length), f32),
            pltpu.VMEM((CTX, 2 * EXP, 2 * length), f32),
            pltpu.VMEM((EXP, 8, 128), f32),
            pltpu.VMEM((EXP, 8, 128), f32),
            pltpu.VMEM((slots, 128), f32),
            pltpu.VMEM((2 * length, 8), f32),
            pltpu.VMEM((CTX, slots, width), kind),
            pltpu.VMEM((units, model), kind),
            pltpu.VMEM((units, model), kind),
            pltpu.VMEM((units, model), kind),
            pltpu.VMEM((2, half_rows, units), f32),
            pltpu.VMEM((2, half_rows, units), f32),
            pltpu.VMEM((2, half_rows, units), kind),
            pltpu.VMEM(blocks, kind),
            pltpu.VMEM(blocks, kind),
            pltpu.VMEM((2, 5, 2, half_rows, width), kind),
            pltpu.VMEM((2, 5, 2, half_rows, width), kind),
            pltpu.VMEM((EXP, PAD, width), kind),
            pltpu.VMEM((EXP, PAD, width), kind),
            dma((3,)), dma((40,)), dma((40,)), dma((40,)), dma((40,)), dma((40,)), dma((40,)),
            dma((4,)), dma((4,)), dma((4,)), dma((4,)), dma((8,)), dma((8,)),
            dma((EXP,)), dma((EXP,)), dma((CTX,)), dma((CTX,)),
            dma((EXP,)), dma((EXP,)), dma((EXP,)), dma((EXP,)),
        ],
        compiler_params=pltpu.CompilerParams(
            collective_id=1, has_side_effects=True, vmem_limit_bytes=62 * 1024 * 1024
        ),
        cost_estimate=pl.CostEstimate(
            flops=6 * slots * model * units, bytes_accessed=6 * model * units, transcendentals=0
        ),
    )(normed, residual, out_weight, router, ids, gate_w, up_w, down_w)


def carried_in(array, axis, combine, identity):
    size, index = (lax.axis_size(axis), lax.axis_index(axis))
    everything = jax.tree.map(
        lambda part, kind: lax.all_gather(part.astype(kind), axis),
        array,
        (jnp.bfloat16, jnp.bfloat16),
    )
    start = jax.tree.map(
        lambda part, zero: jnp.broadcast_to(jnp.asarray(zero, part.dtype), part.shape),
        array,
        identity,
    )

    def step(k, before):
        reached = k < index
        new = combine(
            before, jax.tree.map(lambda part, own: part[k].astype(own.dtype), everything, array)
        )
        return jax.tree.map(lambda a, b: jnp.where(reached, a, b), new, before)

    return lax.fori_loop(0, size, step, start)


def per_device(
    query_rows,
    key_rows,
    value_rows,
    log_decay,
    residual,
    out_weight,
    router_weight,
    expert_ids,
    expert_gate,
    expert_up,
    expert_down,
):
    length = query_rows.shape[0]
    head_count = log_decay.shape[0]
    head_width = query_rows.shape[1] // head_count
    query_heads = query_rows.reshape(length, head_count, head_width)
    key_heads = key_rows.reshape(length, head_count, head_width)
    value_heads = value_rows.reshape(length, head_count, head_width)
    cumulative = jnp.cumsum(log_decay, axis=1)
    row_index = lax.broadcasted_iota(jnp.int32, (length, length), 0)
    col_index = lax.broadcasted_iota(jnp.int32, (length, length), 1)
    gaps = cumulative[:, :, None] - cumulative[:, None, :]
    mask_weights = jnp.where((col_index <= row_index)[None], jnp.exp(jnp.minimum(gaps, 0.0)), 0.0)
    scores = jnp.einsum("thd,shd->hts", query_heads, key_heads, preferred_element_type=jnp.float32)
    scaled_scores = (scores * mask_weights).astype(jnp.bfloat16)
    inside = jnp.einsum(
        "hts,shd->thd", scaled_scores, value_heads, preferred_element_type=jnp.float32
    )
    block_total = cumulative[:, -1]
    keep_factor = jnp.exp(block_total[:, None] - cumulative)
    weighted_keys = key_heads.astype(jnp.float32) * keep_factor.T[:, :, None]
    block_state = jnp.einsum(
        "thd,the->hde", weighted_keys, value_heads.astype(jnp.float32), precision=highest
    )

    def combine_pair(earlier_pair, later_pair):
        merged_total = earlier_pair[0] + later_pair[0]
        merged_state = jnp.exp(later_pair[0])[:, None, None] * earlier_pair[1] + later_pair[1]
        return (merged_total, merged_state)

    empty_pair = (jnp.zeros_like(block_total), jnp.zeros_like(block_state))
    prior_total, prior_state = carried_in(
        (block_total, block_state), "ctx", combine_pair, empty_pair
    )
    outside = jnp.einsum(
        "thd,hde->the", query_heads.astype(jnp.float32), prior_state, precision=highest
    )
    outside = outside * jnp.exp(cumulative).T[:, :, None]
    attended = inside + outside
    normed = attended * lax.rsqrt(jnp.mean(attended * attended, axis=2, keepdims=True) + epsilon)
    normed = normed.astype(jnp.bfloat16).reshape(length, head_count * head_width)
    return project_and_mix(
        normed,
        residual,
        out_weight,
        router_weight.T,
        expert_ids.T,
        expert_gate[0].T,
        expert_up[0].T,
        expert_down[0],
    )


def solution(mesh):
    return jax.shard_map(
        per_device,
        mesh=mesh,
        in_specs=(
            P("ctx", "exp"),
            P("ctx", "exp"),
            P("ctx", "exp"),
            P("exp", "ctx"),
            P("ctx", "exp"),
            P("exp", "ctx"),
            P(),
            P("ctx", None),
            P("exp", None, "ctx"),
            P("exp", None, "ctx"),
            P("exp", "ctx", None),
        ),
        out_specs=(P("ctx", "exp"), P("ctx", "exp")),
        check_vma=False,
    )
```

```python
import jax
import jax.numpy as jnp
from jax import lax
from jax.experimental import pallas as pl
from jax.experimental.pallas import tpu as pltpu
from jax.sharding import PartitionSpec as P

MESH = pl.DeviceIdType.MESH
SIDE = 4
CTX = 16
EXP = 8
PAD = 80
GROUPS = (0, -1, 1, 2)
FAR_FIRST = (2, 1, -1, 0)
BOTH = (0, 1)
epsilon = 1e-05
highest = lax.Precision.HIGHEST


def dot(a, b):
    return jnp.dot(a, b, preferred_element_type=jnp.float32)


def dot_rows(a, b):
    return lax.dot_general(a, b, (((1,), (1,)), ((), ())), preferred_element_type=jnp.float32)


def chunk_at(half, u, v):
    u, v = (u + SIDE) % SIDE, (v + SIDE) % SIDE
    return u * SIDE + v if half == 0 else v * SIDE + u


def plane_device(half, axis, step):
    me = lax.axis_index("ctx")
    y, z = me // SIDE, me % SIDE
    u, v = (y, z) if half == 0 else (z, y)
    return chunk_at(half, u + step, v) if axis == 0 else chunk_at(half, u, v + step)


class Gather:
    def __init__(self, buf, send_sem, recv_sem):
        self.buf, self.send_sem, self.recv_sem = buf, send_sem, recv_sem
        self.half_rows = buf.shape[1] // 2
        me = lax.axis_index("ctx")
        y, z = me // SIDE, me % SIDE
        self.place = ((y, z), (z, y))

    def copy(self, half, ring, kind, step):
        u, v = self.place[half]
        axis = 0 if ring == 0 else 1
        held = (0, 0, -1, 1)[kind] + step
        if axis == 0:
            chunk = chunk_at(half, u + held, v)
        else:
            chunk = chunk_at(half, u + GROUPS[ring - 1], v + held)
        start, size = half * self.half_rows, self.half_rows
        if kind >= 2:
            size = size // 2
            start = start + (kind - 2) * size
        ref = self.buf.at[chunk, pl.ds(start, size)]
        k = (half * 5 + ring) * 4 + kind
        return pltpu.make_async_remote_copy(
            src_ref=ref,
            dst_ref=ref,
            send_sem=self.send_sem.at[k],
            recv_sem=self.recv_sem.at[k],
            device_id={"ctx": plane_device(half, axis, 1 if kind % 2 == 0 else -1)},
            device_id_type=MESH,
        )

    def send(self, half, ring, kind):
        self.copy(half, ring, kind, 0).start()

    def arrive(self, half, ring, kind):
        self.copy(half, ring, kind, -1 if kind % 2 == 0 else 1).wait_recv()

    def begin(self):
        for half in BOTH:
            self.send(half, 0, 0)
            self.send(half, 0, 1)
        for half in BOTH:
            self.send(half, 1, 0)
            self.send(half, 1, 1)

    def first_axis(self):
        for half in BOTH:
            self.arrive(half, 0, 0)
            self.send(half, 0, 2)
            self.arrive(half, 0, 1)
            self.send(half, 0, 3)
        for ring in (2, 3):
            for half in BOTH:
                self.send(half, ring, 0)
                self.send(half, ring, 1)
        for half in BOTH:
            self.arrive(half, 0, 2)
            self.arrive(half, 0, 3)
            self.send(half, 4, 0)
            self.send(half, 4, 1)

    def relay(self, group):
        for half in BOTH:
            self.arrive(half, group + 1, 0)
            self.send(half, group + 1, 2)
            self.arrive(half, group + 1, 1)
            self.send(half, group + 1, 3)

    def settle(self, half, group):
        self.arrive(half, group + 1, 2)
        self.arrive(half, group + 1, 3)

    def drain(self):
        for half in BOTH:
            for ring in range(5):
                for kind in range(4):
                    self.copy(half, ring, kind, 0).wait_send()


class RingSum:
    def __init__(self, rel_out, rel_in, full_out, full_in, send_sem, recv_sem, base, device):
        self.refs = (rel_out, rel_in, full_out, full_in)
        self.send_sem, self.recv_sem, self.base, self.device = send_sem, recv_sem, base, device
        self.sub = rel_out.shape[0] // 2

    def copy(self, kind):
        rel_out, rel_in, full_out, full_in = self.refs
        if kind < 2:
            part = pl.ds(kind * self.sub, self.sub)
            src, dst = rel_out.at[part], rel_in.at[part]
        else:
            src, dst = full_out.at[kind - 2], full_in.at[kind - 2]
        return pltpu.make_async_remote_copy(
            src_ref=src,
            dst_ref=dst,
            send_sem=self.send_sem.at[self.base + kind],
            recv_sem=self.recv_sem.at[self.base + kind],
            device_id=self.device(1 if kind % 2 == 0 else -1),
            device_id_type=MESH,
        )

    def far(self, value):
        rel_out = self.refs[0]
        rel_out[...] = value.astype(rel_out.dtype)
        self.copy(0).start()
        self.copy(1).start()

    def near(self, way, value):
        _, rel_in, full_out, _ = self.refs
        full_out[way] = value.astype(full_out.dtype)
        start = way * self.sub
        part = pl.ds(start, self.sub)
        self.copy(way).wait_recv()
        full_out[way, part] = (
            value[start : start + self.sub] + rel_in[part].astype(jnp.float32)
        ).astype(full_out.dtype)
        self.copy(2 + way).start()

    def total(self, value):
        full_in = self.refs[3]
        for way in BOTH:
            self.copy(2 + way).wait_recv()
            value = value + full_in[way].astype(jnp.float32)
        return value

    def drain(self):
        for kind in range(4):
            self.copy(kind).wait_send()


def layer_kernel(
    query_ref, key_ref, value_ref, decay_ref,
    residual_ref, out_w, router_ref, ids_ref, gate_hbm, up_hbm, down_hbm,
    hidden_ref, mixture_ref,
    fresh_out, fresh_in, prior_out, prior_in, inside, normed_all, pair_out, pair_in, proj_rel_out, proj_rel_in, proj_full_out, proj_full_in,
    res_out, res_in, ids_out, ids_in, hid_out, hid_in, mix_out, mix_in,
    picks, disp_out, disp_in, stat_out, stat_in, scale_out, scale_in, scale_col, token_weight,
    rows, gate_w, up_w, down_w, gate_acc, up_acc, active,
    rel_out, rel_in, full_out, full_in, ret_out, ret_in,
    weight_sem, f_send, f_recv, o_send, o_recv, n_send, n_recv, g_send, g_recv, r_send, r_recv, p_send, p_recv, q_send, q_recv,
    swap_send, swap_recv, d_send, d_recv, s_send, s_recv, c_send, c_recv, b_send, b_recv,
):
    ctx, exp = lax.axis_index("ctx"), lax.axis_index("exp")
    y, z = ctx // SIDE, ctx % SIDE
    x, core = exp // 2, exp % 2
    length, part_width = res_in.shape[1], res_in.shape[2]
    width = rows.shape[2]
    slots = rows.shape[1]
    pair_slots = slots // EXP
    half_rows = slots // 2
    model = down_w.shape[1]
    f32, kind = jnp.float32, rows.dtype
    place = ((y, z), (z, y))

    weight_copies = [
        pltpu.make_async_copy(src, dst, weight_sem.at[i])
        for i, (src, dst) in enumerate(((gate_hbm, gate_w), (up_hbm, up_w), (down_hbm, down_w)))
    ]
    for copy in weight_copies:
        copy.start()

    def partner(i):
        return {"ctx": 2 * exp + i, "exp": ctx // 2}

    def partner_is_me(i):
        return jnp.logical_and(ctx == 2 * exp + i, exp == ctx // 2)

    slot = ctx % 2
    barrier = pltpu.get_barrier_semaphore()

    @pl.loop(1, CTX)
    def _(k):
        pl.semaphore_signal(barrier, inc=1, device_id={"ctx": (ctx + k) % CTX}, device_id_type=MESH)

    @pl.loop(1, EXP)
    def _(k):
        pl.semaphore_signal(barrier, inc=1, device_id={"exp": (exp + k) % EXP}, device_id_type=MESH)

    for i in BOTH:

        @pl.when(jnp.logical_not(partner_is_me(i)))
        def _():
            pl.semaphore_signal(barrier, inc=1, device_id=partner(i), device_id_type=MESH)

    heads = decay_ref.shape[0]
    head = query_ref.shape[1] // heads
    row_index = lax.broadcasted_iota(jnp.int32, (length, length), 0)
    col_index = lax.broadcasted_iota(jnp.int32, (length, length), 1)
    cum_row = jnp.dot(
        decay_ref[...], (row_index <= col_index).astype(f32),
        preferred_element_type=f32, precision=highest,
    )
    cum_col = cum_row.T
    block_total = cum_row[:, length - 1 : length]
    keep = jnp.exp(block_total - cum_row).T
    block_keep = jnp.broadcast_to(jnp.exp(block_total), (heads, head))
    keep_high = block_keep.astype(kind)
    keep_low = (block_keep - keep_high.astype(f32)).astype(kind)
    part_rows = head // 2
    line = lax.broadcasted_iota(jnp.int32, (16, head), 0)
    for h in range(heads):
        lanes = slice(h * head, (h + 1) * head)
        weighted = (key_ref[:, lanes].astype(f32) * keep[:, h : h + 1]).astype(kind)
        state = lax.dot_general(
            weighted, value_ref[:, lanes], (((0,), (0,)), ((), ())), preferred_element_type=f32
        ).astype(kind)
        factor = jnp.where(
            line == 0, keep_high[h : h + 1].astype(f32),
            jnp.where(line == 1, keep_low[h : h + 1].astype(f32), 0.0),
        ).astype(kind)
        for i in BOTH:
            fresh_out[2 * h + i, 0:part_rows] = state[i * part_rows : (i + 1) * part_rows]
            fresh_out[2 * h + i, part_rows : part_rows + 16] = factor
    ids_out[0:2, :] = ids_ref[...]
    for i in BOTH:
        res_out[i] = residual_ref[:, i * part_width : (i + 1) * part_width]
    gate_acc[...] = jnp.zeros_like(gate_acc)
    up_acc[...] = jnp.zeros_like(up_acc)
    pl.semaphore_wait(barrier, CTX + EXP - 2 + jnp.where(exp == ctx // 2, 1, 2))

    def swap(index, i, src, dst, mine):
        def copy(arriving):
            k = 2 * index
            return pltpu.make_async_remote_copy(
                src_ref=src,
                dst_ref=dst.at[i] if arriving else dst.at[slot],
                send_sem=swap_send.at[k + i],
                recv_sem=swap_recv.at[k + i] if arriving else swap_recv.at[k + slot],
                device_id=partner(i),
                device_id_type=MESH,
            )

        def start():
            @pl.when(partner_is_me(i))
            def _():
                mine()

            @pl.when(jnp.logical_not(partner_is_me(i)))
            def _():
                copy(False).start()

        def arrive():
            @pl.when(jnp.logical_not(partner_is_me(i)))
            def _():
                copy(True).wait_recv()

        def drain():
            @pl.when(jnp.logical_not(partner_is_me(i)))
            def _():
                copy(False).wait_send()

        return start, arrive, drain

    def stay(src, i, dst):
        def mine():
            dst[i] = src[i]

        return mine

    def stay_ids(i):
        def mine():
            ids_in[i] = ids_out[...]

        return mine

    def state_copy(k, src_ctx):
        return pltpu.make_async_remote_copy(
            src_ref=fresh_out.at[(ctx + k) % CTX],
            dst_ref=fresh_in.at[src_ctx],
            send_sem=f_send.at[k],
            recv_sem=f_recv.at[k],
            device_id={"ctx": (ctx + k) % CTX},
            device_id_type=MESH,
        )

    def prior_copy(k, src_ctx):
        return pltpu.make_async_remote_copy(
            src_ref=prior_out.at[(ctx + k) % CTX],
            dst_ref=prior_in.at[src_ctx],
            send_sem=o_send.at[k],
            recv_sem=o_recv.at[k],
            device_id={"ctx": (ctx + k) % CTX},
            device_id_type=MESH,
        )

    @pl.loop(1, CTX)
    def _(k):
        state_copy(k, ctx).start()

    fresh_in[ctx] = fresh_out[ctx]
    for h in range(heads):
        lanes = slice(h * head, (h + 1) * head)
        scores = dot_rows(query_ref[:, lanes], key_ref[:, lanes])
        gaps = cum_col[:, h : h + 1] - cum_row[h : h + 1, :]
        decayed = jnp.where(col_index <= row_index, jnp.exp(jnp.minimum(gaps, 0.0)), 0.0)
        inside[:, lanes] = dot((scores * decayed).astype(kind), value_ref[:, lanes])

    @pl.loop(1, CTX)
    def _(k):
        state_copy(k, (ctx + CTX - k) % CTX).wait_recv()

    state = jnp.zeros((part_rows, head), f32)
    for j in range(CTX):
        prior_out[j] = state.astype(kind)
        if j < CTX - 1:
            factor = fresh_in[j, part_rows : part_rows + 16].astype(f32)
            state = (factor[0:1] + factor[1:2]) * state + fresh_in[j, 0:part_rows].astype(f32)

    @pl.loop(1, CTX)
    def _(k):
        prior_copy(k, ctx).start()

    prior_in[ctx] = prior_out[ctx]
    grown = jnp.exp(cum_col)

    @pl.loop(1, CTX)
    def _(k):
        prior_copy(k, (ctx + CTX - k) % CTX).wait_recv()

    for h in range(heads):
        lanes = slice(h * head, (h + 1) * head)
        before_block = prior_in[2 * h : 2 * h + 2].reshape(head, head)
        attended = inside[:, lanes] + dot(query_ref[:, lanes], before_block) * grown[:, h : h + 1]
        square = jnp.mean(attended * attended, axis=1, keepdims=True)
        normed_all[ctx, :, lanes] = (attended * lax.rsqrt(square + epsilon)).astype(kind)

    gather = Gather(normed_all, n_send, n_recv)
    gather.begin()
    swaps_res = [swap(0, i, res_out.at[i], res_in, stay(res_out, i, res_in)) for i in BOTH]
    swaps_ids = [swap(1, i, ids_out, ids_in, stay_ids(i)) for i in BOTH]
    for start, _, _ in swaps_res + swaps_ids:
        start()
    gather.first_axis()
    gather.relay(0)
    gather.relay(1)
    for half in BOTH:
        gather.settle(half, 0)
    gather.relay(2)
    for half in BOTH:
        gather.settle(half, 1)
    gather.relay(3)
    for _, arrive, _ in swaps_ids:
        arrive()

    expert_row = lax.broadcasted_iota(jnp.int32, (EXP, length), 0)
    later = (
        lax.broadcasted_iota(jnp.int32, (length, length), 0)
        < lax.broadcasted_iota(jnp.int32, (length, length), 1)
    ).astype(jnp.bfloat16)
    named = []
    for i in BOTH:
        chosen = [expert_row == ids_in[i, k : k + 1, :] for k in BOTH]
        count = chosen[0].astype(f32) + chosen[1].astype(f32)
        before = dot(count.astype(jnp.bfloat16), later)
        key = jnp.where(count > 0.5, before + float(i * (pair_slots // 2)), -1.0)
        named.append((key, chosen))
    key = jnp.concatenate([named[0][0], named[1][0]], axis=1)
    slot_row = lax.broadcasted_iota(jnp.int32, (128, 2 * length), 0).astype(f32)
    for e in range(EXP):
        picks[e] = jnp.where(slot_row == key[e : e + 1, :], 1.0, 0.0).astype(picks.dtype)

    for group in (2, 3):
        for half in BOTH:
            gather.settle(half, group)

    def project(x_to, core_to):
        blocks = normed_all[pl.ds(2 * (x_to * 2 + core_to), 2)]
        return dot(blocks.reshape(2 * length, blocks.shape[2]), out_w[...])

    def pair_copy(i):
        return pltpu.make_async_remote_copy(
            src_ref=pair_out.at[i],
            dst_ref=pair_in.at[i],
            send_sem=p_send.at[i],
            recv_sem=p_recv.at[i],
            device_id={"exp": x * 2 + 1 - core},
            device_id_type=MESH,
        )

    for i, step in enumerate(FAR_FIRST):
        pair_out[i] = project((x + step + SIDE) % SIDE, 1 - core).astype(kind)
        pair_copy(i).start()
    proj_sum = RingSum(
        proj_rel_out, proj_rel_in, proj_full_out, proj_full_in, q_send, q_recv, 0,
        lambda step: {"exp": ((x + step + SIDE) % SIDE) * 2 + core},
    )
    for i, step in enumerate(FAR_FIRST):
        value = project((x + step + SIDE) % SIDE, core)
        pair_copy(i).wait_recv()
        value = value + pair_in[i].astype(f32)
        if i == 0:
            proj_sum.far(value)
        elif i < 3:
            proj_sum.near(i - 1, value)
        else:
            value = proj_sum.total(value)
    for _, arrive, _ in swaps_res:
        arrive()
    hid = (res_in[...].reshape(2 * length, part_width).astype(f32) + value).astype(kind)
    hid_out[...] = hid.reshape(2, length, part_width)

    def disp_copy(k, src_exp):
        return pltpu.make_async_remote_copy(
            src_ref=disp_out.at[(exp + k) % EXP],
            dst_ref=disp_in.at[src_exp],
            send_sem=d_send.at[k],
            recv_sem=d_recv.at[k],
            device_id={"exp": (exp + k) % EXP},
            device_id_type=MESH,
        )

    @pl.loop(1, EXP)
    def _(k):
        to = (exp + k) % EXP
        disp_out[to] = dot(picks[to, pl.ds(0, PAD), :], hid).astype(kind)
        disp_copy(k, exp).start()

    disp_in[exp] = dot(picks[exp, pl.ds(0, PAD), :], hid).astype(kind)

    swaps_hid = [swap(2, i, hid_out.at[i], hid_in, stay(hid_out, i, hid_in)) for i in BOTH]
    for start, _, _ in swaps_hid:
        start()

    wide = hid.astype(f32)
    columns = pl.ds(pl.multiple_of(ctx * width, width), width)
    stat_out[pl.ds(0, EXP), :] = dot_rows(router_ref[:, columns], hid)
    stat_out[pl.ds(EXP, EXP), :] = lax.dot_general(
        jnp.ones((EXP, width), f32), wide * wide, (((1,), (1,)), ((), ())),
        preferred_element_type=f32, precision=highest,
    )
    stat_in[ctx] = stat_out[...]

    def stat_copy(k, src_ctx):
        return pltpu.make_async_remote_copy(
            src_ref=stat_out,
            dst_ref=stat_in.at[src_ctx],
            send_sem=s_send.at[k],
            recv_sem=s_recv.at[k],
            device_id={"ctx": (ctx + k) % CTX},
            device_id_type=MESH,
        )

    @pl.loop(1, CTX)
    def _(k):
        stat_copy(k, ctx).start()

    @pl.loop(1, EXP)
    def _(k):
        disp_copy(k, (exp + EXP - k) % EXP).wait_recv()

    rows[ctx] = (
        disp_in[...].astype(f32)[:, :pair_slots, :].reshape(slots, width).astype(kind)
    )

    def multiply(half, group):
        u, v = place[half]
        part_rows = pl.ds(half * half_rows, half_rows)

        @pl.loop(0, SIDE)
        def _(i):
            chunk = chunk_at(half, u + GROUPS[group], i)
            part = rows[chunk, part_rows, :]
            depth = pl.ds(pl.multiple_of(chunk * width, width), width)
            gate_acc[half] += dot_rows(part, gate_w[:, depth])
            up_acc[half] += dot_rows(part, up_w[:, depth])

    spread = Gather(rows, g_send, g_recv)
    spread.begin()
    spread.first_axis()
    spread.relay(0)

    @pl.loop(1, CTX)
    def _(k):
        stat_copy(k, (ctx + CTX - k) % CTX).wait_recv()

    stats = stat_in[0]
    for k in range(1, CTX):
        stats = stats + stat_in[k]
    row_scale = lax.rsqrt(stats[EXP:, :] * (1.0 / model) + epsilon)
    logits = stats[:EXP, :] * row_scale
    high = row_scale.astype(jnp.bfloat16).astype(f32)
    middle = (row_scale - high).astype(jnp.bfloat16).astype(f32)
    low = row_scale - high - middle
    which = lax.broadcasted_iota(jnp.int32, row_scale.shape, 0)
    thirds = jnp.where(
        which == 0, high, jnp.where(which == 1, middle, jnp.where(which == 2, low, 0.0))
    ).astype(jnp.bfloat16)

    def scale_copy(k, src_exp):
        return pltpu.make_async_remote_copy(
            src_ref=scale_out.at[(exp + k) % EXP],
            dst_ref=scale_in.at[src_exp],
            send_sem=c_send.at[k],
            recv_sem=c_recv.at[k],
            device_id={"exp": (exp + k) % EXP},
            device_id_type=MESH,
        )

    @pl.loop(1, EXP)
    def _(k):
        to = (exp + k) % EXP
        scale_out[to] = dot_rows(thirds, picks[to])
        scale_copy(k, exp).start()

    scale_in[exp] = dot_rows(thirds, picks[exp])

    picked = []
    for k in BOTH:
        chosen = jnp.concatenate([named[0][1][k], named[1][1][k]], axis=1)
        picked.append(jnp.sum(jnp.where(chosen, logits, 0.0), axis=0, keepdims=True))
    first_weight = 1.0 / (1.0 + jnp.exp(picked[1] - picked[0]))
    second_weight = 1.0 / (1.0 + jnp.exp(picked[0] - picked[1]))
    token_weight[...] = jnp.where(
        which == 0, first_weight, jnp.where(which == 1, second_weight, 0.0)
    ).T

    weight_copies[0].wait()
    weight_copies[1].wait()
    spread.relay(1)
    for half in BOTH:
        spread.settle(half, 0)
        multiply(half, 0)
    spread.relay(2)
    for half in BOTH:
        spread.settle(half, 1)
        multiply(half, 1)
    spread.relay(3)

    @pl.loop(1, EXP)
    def _(k):
        scale_copy(k, (exp + EXP - k) % EXP).wait_recv()

    row_scales = jnp.sum(scale_in[...], axis=1).T
    for e in range(EXP):
        scale_col[pl.ds(e * pair_slots, pair_slots), :] = jnp.broadcast_to(
            row_scales[:pair_slots, e : e + 1], (pair_slots, 128)
        )
    for half in BOTH:
        spread.settle(half, 2)
        multiply(half, 2)
    for half in BOTH:
        spread.settle(half, 3)
        multiply(half, 3)
        scale = scale_col[pl.ds(half * half_rows, half_rows), 0:1]
        gate = gate_acc[half] * scale
        up = up_acc[half] * scale
        active[half] = (gate * (1.0 / (1.0 + jnp.exp(-gate))) * up).astype(kind)
    weight_copies[2].wait()

    def product(half, du, dv):
        u, v = place[half]
        chunk = chunk_at(half, u + dv, v + du)
        return dot(active[half], down_w[:, pl.ds(pl.multiple_of(chunk * width, width), width)])

    def ring_device(half, axis):
        return lambda step: {"ctx": plane_device(half, axis, step)}

    sums = [
        [
            RingSum(
                rel_out.at[half, group], rel_in.at[half, group],
                full_out.at[half, group], full_in.at[half, group],
                r_send, r_recv, (half * 5 + group) * 4, ring_device(half, 1 if group < 4 else 0),
            )
            for group in range(5)
        ]
        for half in BOTH
    ]

    def back_copy(k, src_exp):
        return pltpu.make_async_remote_copy(
            src_ref=ret_out.at[(exp + k) % EXP],
            dst_ref=ret_in.at[src_exp],
            send_sem=b_send.at[k],
            recv_sem=b_recv.at[k],
            device_id={"exp": (exp + k) % EXP},
            device_id_type=MESH,
        )

    for group in range(4):
        for half in BOTH:
            sums[half][group].far(product(half, 2, FAR_FIRST[group]))
    for group in range(4):
        for half in BOTH:
            sums[half][group].near(0, product(half, 1, FAR_FIRST[group]))
            sums[half][group].near(1, product(half, -1, FAR_FIRST[group]))
    blank = jnp.zeros((PAD - pair_slots, width), f32)
    for group in range(4):
        for half in BOTH:
            value = sums[half][group].total(product(half, 0, FAR_FIRST[group]))
            if group == 0:
                sums[half][4].far(value)
            elif group < 3:
                sums[half][4].near(group - 1, value)
            else:
                value = sums[half][4].total(value)
                for i in range(EXP // 2):
                    part = value[i * pair_slots : (i + 1) * pair_slots]
                    ret_out[half * (EXP // 2) + i] = jnp.concatenate([part, blank], axis=0).astype(kind)

    @pl.loop(1, EXP)
    def _(k):
        back_copy(k, exp).start()

    ret_in[exp] = ret_out[exp]

    @pl.loop(1, EXP)
    def _(k):
        back_copy(k, (exp + EXP - k) % EXP).wait_recv()

    back = ret_in[...].reshape(EXP * PAD, width)
    weighted = []
    for k in BOTH:
        chosen = jnp.concatenate([named[0][1][k], named[1][1][k]], axis=1)
        take = jnp.concatenate(
            [
                jnp.where(chosen[e : e + 1, :], picks[e, pl.ds(0, PAD), :].astype(f32), 0.0)
                for e in range(EXP)
            ],
            axis=0,
        ).T.astype(kind)
        weighted.append((dot(take, back) * token_weight[:, k : k + 1]).astype(kind).astype(f32))
    mix_out[...] = (weighted[0] + weighted[1]).astype(kind).reshape(2, length, part_width)
    swaps_mix = [swap(3, i, mix_out.at[i], mix_in, stay(mix_out, i, mix_in)) for i in BOTH]
    for start, _, _ in swaps_mix:
        start()
    for _, arrive, _ in swaps_hid + swaps_mix:
        arrive()
    for i in BOTH:
        hidden_ref[:, i * part_width : (i + 1) * part_width] = hid_in[i]
        mixture_ref[:, i * part_width : (i + 1) * part_width] = mix_in[i]

    gather.drain()
    spread.drain()
    proj_sum.drain()
    for i in range(4):
        pair_copy(i).wait_send()
    for half in BOTH:
        for group in range(5):
            sums[half][group].drain()
    for _, _, drain in swaps_res + swaps_ids + swaps_hid + swaps_mix:
        drain()

    @pl.loop(1, EXP)
    def _(k):
        disp_copy(k, exp).wait_send()
        scale_copy(k, exp).wait_send()
        back_copy(k, exp).wait_send()

    @pl.loop(1, CTX)
    def _(k):
        stat_copy(k, ctx).wait_send()
        state_copy(k, ctx).wait_send()
        prior_copy(k, ctx).wait_send()


def layer(query, key, value, decay, residual, out_weight, router, ids, gate_w, up_w, down_w):
    length, inner = query.shape
    head = inner // decay.shape[0]
    width = out_weight.shape[1]
    units, model = down_w.shape
    slots = CTX * (2 * length // EXP + length // 32)
    half_rows = slots // 2
    kind, f32 = query.dtype, jnp.float32
    vmem = pl.BlockSpec(memory_space=pltpu.VMEM)
    anywhere = pl.BlockSpec(memory_space=pl.ANY)
    two = (2, length, width)
    dma = pltpu.SemaphoreType.DMA
    out = jax.ShapeDtypeStruct(residual.shape, kind)
    blocks = (2, 5, half_rows, width)
    return pl.pallas_call(
        layer_kernel,
        out_shape=(out, out),
        in_specs=[vmem] * 8 + [anywhere] * 3,
        out_specs=(vmem, vmem),
        scratch_shapes=[
            pltpu.VMEM((CTX, head // 2 + 16, head), kind),
            pltpu.VMEM((CTX, head // 2 + 16, head), kind),
            pltpu.VMEM((CTX, head // 2, head), kind),
            pltpu.VMEM((CTX, head // 2, head), kind),
            pltpu.VMEM((length, inner), f32),
            pltpu.VMEM((CTX, length, inner), kind),
            pltpu.VMEM((4, 2 * length, width), kind),
            pltpu.VMEM((4, 2 * length, width), kind),
            pltpu.VMEM((2 * length, width), kind),
            pltpu.VMEM((2 * length, width), kind),
            pltpu.VMEM((2, 2 * length, width), kind),
            pltpu.VMEM((2, 2 * length, width), kind),
            pltpu.VMEM(two, kind),
            pltpu.VMEM(two, kind),
            pltpu.VMEM((8, length), jnp.int32),
            pltpu.VMEM((2, 8, length), jnp.int32),
            pltpu.VMEM(two, kind),
            pltpu.VMEM(two, kind),
            pltpu.VMEM(two, kind),
            pltpu.VMEM(two, kind),
            pltpu.VMEM((EXP, 128, 2 * length), kind),
            pltpu.VMEM((EXP, PAD, width), kind),
            pltpu.VMEM((EXP, PAD, width), kind),
            pltpu.VMEM((2 * EXP, 2 * length), f32),
            pltpu.VMEM((CTX, 2 * EXP, 2 * length), f32),
            pltpu.VMEM((EXP, 8, 128), f32),
            pltpu.VMEM((EXP, 8, 128), f32),
            pltpu.VMEM((slots, 128), f32),
            pltpu.VMEM((2 * length, 8), f32),
            pltpu.VMEM((CTX, slots, width), kind),
            pltpu.VMEM((units, model), kind),
            pltpu.VMEM((units, model), kind),
            pltpu.VMEM((units, model), kind),
            pltpu.VMEM((2, half_rows, units), f32),
            pltpu.VMEM((2, half_rows, units), f32),
            pltpu.VMEM((2, half_rows, units), kind),
            pltpu.VMEM(blocks, kind),
            pltpu.VMEM(blocks, kind),
            pltpu.VMEM((2, 5, 2, half_rows, width), kind),
            pltpu.VMEM((2, 5, 2, half_rows, width), kind),
            pltpu.VMEM((EXP, PAD, width), kind),
            pltpu.VMEM((EXP, PAD, width), kind),
            dma((3,)), dma((CTX,)), dma((CTX,)), dma((CTX,)), dma((CTX,)), dma((40,)), dma((40,)), dma((40,)), dma((40,)), dma((40,)), dma((40,)),
            dma((4,)), dma((4,)), dma((4,)), dma((4,)), dma((8,)), dma((8,)),
            dma((EXP,)), dma((EXP,)), dma((CTX,)), dma((CTX,)),
            dma((EXP,)), dma((EXP,)), dma((EXP,)), dma((EXP,)),
        ],
        compiler_params=pltpu.CompilerParams(
            collective_id=1, has_side_effects=True, vmem_limit_bytes=62 * 1024 * 1024
        ),
        cost_estimate=pl.CostEstimate(
            flops=6 * slots * model * units, bytes_accessed=6 * model * units, transcendentals=0
        ),
    )(query, key, value, decay, residual, out_weight, router, ids, gate_w, up_w, down_w)


def per_device(
    query_rows,
    key_rows,
    value_rows,
    log_decay,
    residual,
    out_weight,
    router_weight,
    expert_ids,
    expert_gate,
    expert_up,
    expert_down,
):
    return layer(
        query_rows,
        key_rows,
        value_rows,
        log_decay,
        residual,
        out_weight,
        router_weight.T,
        expert_ids.T,
        expert_gate[0].T,
        expert_up[0].T,
        expert_down[0],
    )


def solution(mesh):
    return jax.shard_map(
        per_device,
        mesh=mesh,
        in_specs=(
            P("ctx", "exp"),
            P("ctx", "exp"),
            P("ctx", "exp"),
            P("exp", "ctx"),
            P("ctx", "exp"),
            P("exp", "ctx"),
            P(),
            P("ctx", None),
            P("exp", None, "ctx"),
            P("exp", None, "ctx"),
            P("exp", "ctx", None),
        ),
        out_specs=(P("ctx", "exp"), P("ctx", "exp")),
        check_vma=False,
    )
```

```python
import jax
import jax.numpy as jnp
from jax import lax
from jax.experimental import pallas as pl
from jax.experimental.pallas import tpu as pltpu
from jax.sharding import PartitionSpec as P

MESH = pl.DeviceIdType.MESH
SIDE = 4
CTX = 16
EXP = 8
PAD = 80
BACK = 48
GROUPS = (0, -1, 1, 2)
FAR_FIRST = (2, 1, -1, 0)
BOTH = (0, 1)
epsilon = 1e-05
highest = lax.Precision.HIGHEST


def dot(a, b):
    return jnp.dot(a, b, preferred_element_type=jnp.float32)


def dot_rows(a, b):
    return lax.dot_general(a, b, (((1,), (1,)), ((), ())), preferred_element_type=jnp.float32)


def chunk_at(half, u, v):
    u, v = (u + SIDE) % SIDE, (v + SIDE) % SIDE
    return u * SIDE + v if half == 0 else v * SIDE + u


def plane_device(half, axis, step):
    me = lax.axis_index("ctx")
    y, z = me // SIDE, me % SIDE
    u, v = (y, z) if half == 0 else (z, y)
    return chunk_at(half, u + step, v) if axis == 0 else chunk_at(half, u, v + step)


class Gather:
    def __init__(self, buf, send_sem, recv_sem):
        self.buf, self.send_sem, self.recv_sem = buf, send_sem, recv_sem
        self.half_rows = buf.shape[1] // 2
        me = lax.axis_index("ctx")
        y, z = me // SIDE, me % SIDE
        self.place = ((y, z), (z, y))

    def copy(self, half, ring, kind, step):
        u, v = self.place[half]
        axis = 0 if ring == 0 else 1
        held = (0, 0, -1, 1)[kind] + step
        if axis == 0:
            chunk = chunk_at(half, u + held, v)
        else:
            chunk = chunk_at(half, u + GROUPS[ring - 1], v + held)
        start, size = half * self.half_rows, self.half_rows
        if kind >= 2:
            size = size // 2
            start = start + (kind - 2) * size
        ref = self.buf.at[chunk, pl.ds(start, size)]
        k = (half * 5 + ring) * 4 + kind
        return pltpu.make_async_remote_copy(
            src_ref=ref,
            dst_ref=ref,
            send_sem=self.send_sem.at[k],
            recv_sem=self.recv_sem.at[k],
            device_id={"ctx": plane_device(half, axis, 1 if kind % 2 == 0 else -1)},
            device_id_type=MESH,
        )

    def send(self, half, ring, kind):
        self.copy(half, ring, kind, 0).start()

    def arrive(self, half, ring, kind):
        self.copy(half, ring, kind, -1 if kind % 2 == 0 else 1).wait_recv()

    def blocks(self, ring):
        for half in BOTH:
            self.send(half, ring, 0)
            self.send(half, ring, 1)

    def relay(self, ring):
        for half in BOTH:
            self.arrive(half, ring, 0)
            self.send(half, ring, 2)
            self.arrive(half, ring, 1)
            self.send(half, ring, 3)

    def settle(self, ring):
        for half in BOTH:
            self.arrive(half, ring, 2)
            self.arrive(half, ring, 3)

    def drain(self):
        for half in BOTH:
            for ring in range(5):
                for kind in range(4):
                    self.copy(half, ring, kind, 0).wait_send()


class RingSum:
    def __init__(self, rel_out, rel_in, full_out, full_in, send_sem, recv_sem, base, device):
        self.refs = (rel_out, rel_in, full_out, full_in)
        self.send_sem, self.recv_sem, self.base, self.device = send_sem, recv_sem, base, device
    def copy(self, kind):
        rel_out, rel_in, full_out, full_in = self.refs
        if kind < 2:
            src, dst = rel_out.at[kind], rel_in.at[kind]
        else:
            src, dst = full_out.at[kind - 2], full_in.at[kind - 2]
        return pltpu.make_async_remote_copy(
            src_ref=src,
            dst_ref=dst,
            send_sem=self.send_sem.at[self.base + kind],
            recv_sem=self.recv_sem.at[self.base + kind],
            device_id=self.device(1 if kind % 2 == 0 else -1),
            device_id_type=MESH,
        )

    def far(self, value):
        rel_out = self.refs[0]
        rel_out[...] = value.astype(rel_out.dtype)
        self.copy(0).start()
        self.copy(1).start()

    def near(self, way, value):
        _, rel_in, full_out, _ = self.refs
        full_out[way] = value.astype(full_out.dtype)
        self.copy(way).wait_recv()
        full_out[way, way] = (value[way] + rel_in[way].astype(jnp.float32)).astype(full_out.dtype)
        self.copy(2 + way).start()

    def total(self, value):
        full_in = self.refs[3]
        for way in BOTH:
            self.copy(2 + way).wait_recv()
            value = value + full_in[way].astype(jnp.float32)
        return value

    def drain(self):
        for kind in range(4):
            self.copy(kind).wait_send()


def layer_kernel(
    query_ref, key_ref, value_ref, decay_ref,
    residual_ref, out_w, router_ref, ids_ref, gate_hbm, up_hbm, down_hbm,
    hidden_ref, mixture_ref,
    fresh_out, fresh_in, prior_out, prior_in, inside, normed_all, pair_out, pair_in, proj_rel_out, proj_rel_in, proj_full_out, proj_full_in,
    res_out, res_in, ids_out, ids_in, hid_out, hid_in, share_out, share_in,
    picks, disp_out, disp_in, stat_out, stat_in, scale_out, scale_in, scale_col,
    takes, rows, hidden_w, down_w, hidden_acc, active,
    rel_out, rel_in, full_out, full_in, ret_out, ret_in,
    weight_sem, f_send, f_recv, o_send, o_recv, n_send, n_recv, g_send, g_recv, r_send, r_recv, p_send, p_recv, q_send, q_recv,
    swap_send, swap_recv, d_send, d_recv, s_send, s_recv, c_send, c_recv, b_send, b_recv,
):
    ctx, exp = lax.axis_index("ctx"), lax.axis_index("exp")
    y, z = ctx // SIDE, ctx % SIDE
    x, core = exp // 2, exp % 2
    length, part_width = res_in.shape[1], res_in.shape[2]
    width = rows.shape[2]
    slots = rows.shape[1]
    pair_slots = slots // EXP
    half_rows = slots // 2
    model = down_w.shape[1]
    f32, kind = jnp.float32, rows.dtype
    units = down_w.shape[0]
    place = ((y, z), (z, y))

    weight_copies = [
        pltpu.make_async_copy(src, dst, weight_sem.at[i])
        for i, (src, dst) in enumerate(
            (
                (gate_hbm, hidden_w.at[pl.ds(0, units)]),
                (up_hbm, hidden_w.at[pl.ds(units, units)]),
                (down_hbm, down_w),
            )
        )
    ]
    for copy in weight_copies:
        copy.start()

    def partner(i):
        return {"ctx": 2 * exp + i, "exp": ctx // 2}

    def partner_is_me(i):
        return jnp.logical_and(ctx == 2 * exp + i, exp == ctx // 2)

    slot = ctx % 2
    barrier = pltpu.get_barrier_semaphore()

    @pl.loop(1, CTX)
    def _(k):
        pl.semaphore_signal(barrier, inc=1, device_id={"ctx": (ctx + k) % CTX}, device_id_type=MESH)

    @pl.loop(1, EXP)
    def _(k):
        pl.semaphore_signal(barrier, inc=1, device_id={"exp": (exp + k) % EXP}, device_id_type=MESH)

    for i in BOTH:

        @pl.when(jnp.logical_not(partner_is_me(i)))
        def _():
            pl.semaphore_signal(barrier, inc=1, device_id=partner(i), device_id_type=MESH)

    heads = decay_ref.shape[0]
    head = query_ref.shape[1] // heads
    row_index = lax.broadcasted_iota(jnp.int32, (length, length), 0)
    col_index = lax.broadcasted_iota(jnp.int32, (length, length), 1)
    cum_row = jnp.dot(
        decay_ref[...], (row_index <= col_index).astype(f32),
        preferred_element_type=f32, precision=highest,
    )
    cum_col = cum_row.T
    block_total = cum_row[:, length - 1 : length]
    keep = jnp.exp(block_total - cum_row).T
    block_keep = jnp.broadcast_to(jnp.exp(block_total), (heads, head))
    keep_high = block_keep.astype(kind)
    keep_low = (block_keep - keep_high.astype(f32)).astype(kind)
    part_rows = head // 2
    line = lax.broadcasted_iota(jnp.int32, (16, head), 0)
    for h in range(heads):
        lanes = slice(h * head, (h + 1) * head)
        weighted = (key_ref[:, lanes].astype(f32) * keep[:, h : h + 1]).astype(kind)
        state = lax.dot_general(
            weighted, value_ref[:, lanes], (((0,), (0,)), ((), ())), preferred_element_type=f32
        ).astype(kind)
        factor = jnp.where(
            line == 0, keep_high[h : h + 1].astype(f32),
            jnp.where(line == 1, keep_low[h : h + 1].astype(f32), 0.0),
        ).astype(kind)
        for i in BOTH:
            fresh_out[2 * h + i, 0:part_rows] = state[i * part_rows : (i + 1) * part_rows]
            fresh_out[2 * h + i, part_rows : part_rows + 16] = factor
    def back_origin(i, k):
        return {"ctx": y * SIDE + 2 * core + i, "exp": k}

    def back_from_me(i, k):
        return jnp.logical_and(2 * core + i == z, k == exp)

    for i in BOTH:

        @pl.loop(0, EXP)
        def _(k):
            @pl.when(jnp.logical_not(back_from_me(i, k)))
            def _():
                pl.semaphore_signal(barrier, inc=1, device_id=back_origin(i, k), device_id_type=MESH)

    ids_out[0:2, :] = ids_ref[...]
    for i in BOTH:
        res_out[i] = residual_ref[:, i * part_width : (i + 1) * part_width]
    pl.semaphore_wait(
        barrier,
        CTX + EXP - 2 + jnp.where(exp == ctx // 2, 1, 2) + jnp.where(z // 2 == core, 15, 16),
    )

    def swap(index, i, src, dst, mine):
        def copy(arriving):
            k = 2 * index
            return pltpu.make_async_remote_copy(
                src_ref=src,
                dst_ref=dst.at[i] if arriving else dst.at[slot],
                send_sem=swap_send.at[k + i],
                recv_sem=swap_recv.at[k + i] if arriving else swap_recv.at[k + slot],
                device_id=partner(i),
                device_id_type=MESH,
            )

        def start():
            @pl.when(partner_is_me(i))
            def _():
                mine()

            @pl.when(jnp.logical_not(partner_is_me(i)))
            def _():
                copy(False).start()

        def arrive():
            @pl.when(jnp.logical_not(partner_is_me(i)))
            def _():
                copy(True).wait_recv()

        def drain():
            @pl.when(jnp.logical_not(partner_is_me(i)))
            def _():
                copy(False).wait_send()

        return start, arrive, drain

    def stay(src, i, dst):
        def mine():
            dst[i] = src[i]

        return mine

    def stay_ids(i):
        def mine():
            ids_in[i] = ids_out[...]

        return mine

    def state_copy(k, src_ctx):
        return pltpu.make_async_remote_copy(
            src_ref=fresh_out.at[(ctx + k) % CTX],
            dst_ref=fresh_in.at[src_ctx],
            send_sem=f_send.at[k],
            recv_sem=f_recv.at[k],
            device_id={"ctx": (ctx + k) % CTX},
            device_id_type=MESH,
        )

    def prior_copy(k, src_ctx):
        return pltpu.make_async_remote_copy(
            src_ref=prior_out.at[(ctx + k) % CTX],
            dst_ref=prior_in.at[src_ctx],
            send_sem=o_send.at[k],
            recv_sem=o_recv.at[k],
            device_id={"ctx": (ctx + k) % CTX},
            device_id_type=MESH,
        )

    @pl.loop(1, CTX)
    def _(k):
        state_copy(k, ctx).start()

    fresh_in[ctx] = fresh_out[ctx]
    for h in range(heads):
        lanes = slice(h * head, (h + 1) * head)
        scores = dot_rows(query_ref[:, lanes], key_ref[:, lanes])
        gaps = cum_col[:, h : h + 1] - cum_row[h : h + 1, :]
        decayed = jnp.where(col_index <= row_index, jnp.exp(jnp.minimum(gaps, 0.0)), 0.0)
        inside[:, lanes] = dot((scores * decayed).astype(kind), value_ref[:, lanes])

    @pl.loop(1, CTX)
    def _(k):
        state_copy(k, (ctx + CTX - k) % CTX).wait_recv()

    state = jnp.zeros((part_rows, head), f32)
    for j in range(CTX):
        prior_out[j] = state.astype(kind)
        if j < CTX - 1:
            factor = fresh_in[j, part_rows : part_rows + 16].astype(f32)
            state = (factor[0:1] + factor[1:2]) * state + fresh_in[j, 0:part_rows].astype(f32)

    @pl.loop(1, CTX)
    def _(k):
        prior_copy(k, ctx).start()

    prior_in[ctx] = prior_out[ctx]
    grown = jnp.exp(cum_col)
    hidden_acc[...] = jnp.zeros_like(hidden_acc)

    expert_row = lax.broadcasted_iota(jnp.int32, (EXP, length), 0)
    later = (
        lax.broadcasted_iota(jnp.int32, (length, length), 0)
        < lax.broadcasted_iota(jnp.int32, (length, length), 1)
    ).astype(jnp.bfloat16)

    def slots_of(ids):
        chosen = [expert_row == ids[k : k + 1, :] for k in BOTH]
        count = chosen[0].astype(f32) + chosen[1].astype(f32)
        return chosen, count, dot(count.astype(jnp.bfloat16), later)

    chosen, _, before = slots_of(ids_ref[...])
    first_back = before + (expert_row * BACK).astype(f32)
    spot = [jnp.sum(jnp.where(pick, first_back, 0.0), axis=0, keepdims=True) for pick in chosen]
    spot_col = jnp.where(expert_row == 0, spot[0], jnp.where(expert_row == 1, spot[1], 0.0)).T
    back_row = lax.broadcasted_iota(jnp.int32, (length, EXP * BACK), 1).astype(f32)
    for k in BOTH:
        takes[k] = jnp.where(back_row == spot_col[:, k : k + 1], 1.0, 0.0).astype(kind)

    @pl.loop(1, CTX)
    def _(k):
        prior_copy(k, (ctx + CTX - k) % CTX).wait_recv()

    for h in range(heads):
        lanes = slice(h * head, (h + 1) * head)
        before_block = prior_in[2 * h : 2 * h + 2].reshape(head, head)
        attended = inside[:, lanes] + dot(query_ref[:, lanes], before_block) * grown[:, h : h + 1]
        square = jnp.mean(attended * attended, axis=1, keepdims=True)
        normed_all[ctx, :, lanes] = (attended * lax.rsqrt(square + epsilon)).astype(kind)

    gather = Gather(normed_all, n_send, n_recv)
    gather.blocks(0)
    gather.blocks(1)
    swaps_res = [swap(0, i, res_out.at[i], res_in, stay(res_out, i, res_in)) for i in BOTH]
    swaps_ids = [swap(1, i, ids_out, ids_in, stay_ids(i)) for i in BOTH]
    for start, _, _ in swaps_res + swaps_ids:
        start()
    gather.relay(0)
    gather.blocks(2)
    gather.blocks(3)
    gather.settle(0)
    gather.blocks(4)
    for ring in range(1, 5):
        gather.relay(ring)
    for _, arrive, _ in swaps_ids:
        arrive()

    named = []
    for i in BOTH:
        chosen, count, before = slots_of(ids_in[i])
        key = jnp.where(count > 0.5, before + float(i * (pair_slots // 2)), -1.0)
        named.append((key, chosen))
    key = jnp.concatenate([named[0][0], named[1][0]], axis=1)
    slot_row = lax.broadcasted_iota(jnp.int32, (128, 2 * length), 0).astype(f32)
    for e in range(EXP):
        picks[e] = jnp.where(slot_row == key[e : e + 1, :], 1.0, 0.0).astype(picks.dtype)

    for ring in range(1, 5):
        gather.settle(ring)

    def project(x_to, core_to):
        blocks = normed_all[pl.ds(2 * (x_to * 2 + core_to), 2)]
        return dot(blocks.reshape(2 * length, blocks.shape[2]), out_w[...]).reshape(
            2, length, width
        )

    def pair_copy(i):
        return pltpu.make_async_remote_copy(
            src_ref=pair_out.at[i],
            dst_ref=pair_in.at[i],
            send_sem=p_send.at[i],
            recv_sem=p_recv.at[i],
            device_id={"exp": x * 2 + 1 - core},
            device_id_type=MESH,
        )

    for i, step in enumerate(FAR_FIRST):
        pair_out[i] = project((x + step + SIDE) % SIDE, 1 - core).astype(kind)
        pair_copy(i).start()
    proj_sum = RingSum(
        proj_rel_out, proj_rel_in, proj_full_out, proj_full_in, q_send, q_recv, 0,
        lambda step: {"exp": ((x + step + SIDE) % SIDE) * 2 + core},
    )
    for i, step in enumerate(FAR_FIRST):
        value = project((x + step + SIDE) % SIDE, core)
        pair_copy(i).wait_recv()
        value = value + pair_in[i].astype(f32)
        if i == 0:
            proj_sum.far(value)
        elif i < 3:
            proj_sum.near(i - 1, value)
        else:
            value = proj_sum.total(value)
    for _, arrive, _ in swaps_res:
        arrive()
    hid_out[...] = (res_in[...].astype(f32) + value).astype(kind)
    hid = hid_out[...].reshape(2 * length, width)

    def disp_copy(k, src_exp):
        return pltpu.make_async_remote_copy(
            src_ref=disp_out.at[(exp + k) % EXP],
            dst_ref=disp_in.at[src_exp],
            send_sem=d_send.at[k],
            recv_sem=d_recv.at[k],
            device_id={"exp": (exp + k) % EXP},
            device_id_type=MESH,
        )

    for k in (4, 3, 5, 2, 6, 7, 1):
        to = (exp + k) % EXP
        disp_out[to] = dot(picks[to, pl.ds(0, PAD), :], hid).astype(kind)
        disp_copy(k, exp).start()

    disp_in[exp] = dot(picks[exp, pl.ds(0, PAD), :], hid).astype(kind)

    @pl.loop(1, EXP)
    def _(k):
        disp_copy(k, (exp + EXP - k) % EXP).wait_recv()

    rows[ctx] = (
        disp_in[...].astype(f32)[:, :pair_slots, :].reshape(slots, width).astype(kind)
    )

    def multiply(group, halves=BOTH):
        for half in halves:
            u, v = place[half]
            chunks = [chunk_at(half, u + GROUPS[group], i) for i in range(SIDE)]
            part_rows = pl.ds(half * half_rows, half_rows)
            left = [rows[chunk, part_rows, :] for chunk in chunks]
            right = [
                hidden_w[:, pl.ds(pl.multiple_of(chunk * width, width), width)] for chunk in chunks
            ]
            hidden_acc[half] += dot_rows(
                jnp.concatenate(left, axis=1), jnp.concatenate(right, axis=1)
            )

    spread = Gather(rows, g_send, g_recv)
    spread.blocks(0)
    spread.blocks(1)

    swaps_hid = [swap(2, i, hid_out.at[i], hid_in, stay(hid_out, i, hid_in)) for i in BOTH]
    for start, _, _ in swaps_hid:
        start()

    wide = hid.astype(f32)
    columns = pl.ds(pl.multiple_of(ctx * width, width), width)
    stat_out[pl.ds(0, EXP), :] = dot_rows(router_ref[:, columns], hid)
    square = jnp.sum(wide * wide, axis=1, keepdims=True)
    stat_out[pl.ds(EXP, EXP), :] = jnp.broadcast_to(square, (2 * length, 128)).T[:EXP]
    stat_in[ctx] = stat_out[...]

    def stat_copy(k, src_ctx):
        return pltpu.make_async_remote_copy(
            src_ref=stat_out,
            dst_ref=stat_in.at[src_ctx],
            send_sem=s_send.at[k],
            recv_sem=s_recv.at[k],
            device_id={"ctx": (ctx + k) % CTX},
            device_id_type=MESH,
        )

    @pl.loop(1, CTX)
    def _(k):
        stat_copy(k, ctx).start()

    spread.relay(0)
    spread.settle(0)
    spread.blocks(2)
    spread.relay(1)
    spread.blocks(3)

    weight_copies[0].wait()
    weight_copies[1].wait()
    spread.settle(1)
    spread.relay(2)
    multiply(0)
    spread.blocks(4)
    @pl.loop(1, CTX)
    def _(k):
        stat_copy(k, (ctx + CTX - k) % CTX).wait_recv()

    stats = stat_in[0]
    for k in range(1, CTX):
        stats = stats + stat_in[k]
    row_scale = lax.rsqrt(stats[EXP:, :] * (1.0 / model) + epsilon)
    logits = stats[:EXP, :] * row_scale
    high = row_scale.astype(jnp.bfloat16).astype(f32)
    middle = (row_scale - high).astype(jnp.bfloat16).astype(f32)
    low = row_scale - high - middle
    which = lax.broadcasted_iota(jnp.int32, row_scale.shape, 0)
    thirds = jnp.where(
        which == 0, high, jnp.where(which == 1, middle, jnp.where(which == 2, low, 0.0))
    ).astype(jnp.bfloat16)

    def scale_copy(k, src_exp):
        return pltpu.make_async_remote_copy(
            src_ref=scale_out.at[(exp + k) % EXP],
            dst_ref=scale_in.at[src_exp],
            send_sem=c_send.at[k],
            recv_sem=c_recv.at[k],
            device_id={"exp": (exp + k) % EXP},
            device_id_type=MESH,
        )

    slot_scale = dot_rows(thirds, picks[...].reshape(EXP * 128, 2 * length))
    for e in range(EXP):
        scale_out[e] = slot_scale[:, e * 128 : (e + 1) * 128]

    @pl.loop(1, EXP)
    def _(k):
        scale_copy(k, exp).start()

    scale_in[exp] = scale_out[exp]

    picked = []
    for k in BOTH:
        chosen = jnp.concatenate([named[0][1][k], named[1][1][k]], axis=1)
        picked.append(jnp.sum(jnp.where(chosen, logits, 0.0), axis=0, keepdims=True))
    first_weight = 1.0 / (1.0 + jnp.exp(picked[1] - picked[0]))
    second_weight = 1.0 / (1.0 + jnp.exp(picked[0] - picked[1]))
    share = jnp.where(which == 0, first_weight, jnp.where(which == 1, second_weight, 0.0))
    for i in BOTH:
        share_out[i] = share[:, i * length : (i + 1) * length]
    swaps_share = [swap(3, i, share_out.at[i], share_in, stay(share_out, i, share_in)) for i in BOTH]
    for start, _, _ in swaps_share:
        start()

    spread.settle(2)
    spread.relay(3)
    multiply(1)
    spread.settle(3)
    spread.relay(4)
    multiply(2)

    @pl.loop(1, EXP)
    def _(k):
        scale_copy(k, (exp + EXP - k) % EXP).wait_recv()

    row_scales = jnp.sum(scale_in[...], axis=1).T
    for e in range(EXP):
        scale_col[pl.ds(e * pair_slots, pair_slots), :] = jnp.broadcast_to(
            row_scales[:pair_slots, e : e + 1], (pair_slots, 128)
        )
    weight_copies[2].wait()
    spread.settle(4)

    row_blocks = slots // SIDE

    def product(half, du, dv):
        u, v = place[half]
        to = chunk_at(half, u + dv, v + du)
        to_y, to_z = to // SIDE, to % SIDE
        left = active[pl.ds(pl.multiple_of(to_y * row_blocks, 16), row_blocks), :]
        out = []
        for i in BOTH:
            start = pl.multiple_of(((half * 2 + i) * SIDE + to_z) * width, width)
            out.append(dot(left, down_w[:, pl.ds(start, width)]))
        return jnp.stack(out)

    def ring_device(half, axis):
        return lambda step: {"ctx": plane_device(half, axis, step)}

    sums = [
        [
            RingSum(
                rel_out.at[half, group], rel_in.at[half, group],
                full_out.at[half, group], full_in.at[half, group],
                r_send, r_recv, (half * 5 + group) * 4, ring_device(half, 1 if group < 4 else 0),
            )
            for group in range(5)
        ]
        for half in BOTH
    ]

    def back_copy(m):
        to_exp = 2 * (m // SIDE) + z // 2
        return pltpu.make_async_remote_copy(
            src_ref=ret_out.at[m],
            dst_ref=ret_in.at[z % 2, exp],
            send_sem=b_send.at[m],
            recv_sem=b_recv.at[(z % 2) * EXP + exp],
            device_id={"ctx": y * SIDE + m % SIDE, "exp": to_exp},
            device_id_type=MESH,
        )

    def back_arrival(i, k):
        return pltpu.make_async_remote_copy(
            src_ref=ret_out.at[0],
            dst_ref=ret_in.at[i, k],
            send_sem=b_send.at[0],
            recv_sem=b_recv.at[i * EXP + k],
            device_id=back_origin(i, k),
            device_id_type=MESH,
        )

    def back_is_mine(m):
        return jnp.logical_and(m % SIDE == z, 2 * (m // SIDE) + z // 2 == exp)

    for half in BOTH:
        multiply(3, (half,))
        scale = scale_col[pl.ds(half * half_rows, half_rows), 0:1]
        gate = hidden_acc[half, :, :units] * scale
        up = hidden_acc[half, :, units:] * scale
        active[pl.ds(half * half_rows, half_rows), :] = (
            gate * (1.0 / (1.0 + jnp.exp(-gate))) * up
        ).astype(kind)
    for half in BOTH:
        for group in range(4):
            sums[half][group].far(product(half, 2, FAR_FIRST[group]))
    for group in range(4):
        for half in BOTH:
            sums[half][group].near(0, product(half, 1, FAR_FIRST[group]))
            sums[half][group].near(1, product(half, -1, FAR_FIRST[group]))
    for _, arrive, _ in swaps_hid:
        arrive()
    for i in BOTH:
        hidden_ref[:, i * part_width : (i + 1) * part_width] = hid_in[i]
    block_slots = pair_slots // 2
    blank = jnp.zeros((BACK - block_slots, width), f32)
    for group in range(4):
        for half in BOTH:
            value = sums[half][group].total(product(half, 0, FAR_FIRST[group]))
            if group == 0:
                sums[half][4].far(value)
            elif group < 3:
                sums[half][4].near(group - 1, value)
            else:
                value = sums[half][4].total(value)
                for m in range(half * EXP, half * EXP + EXP):
                    start = m % SIDE * block_slots
                    part = value[m // SIDE - 2 * half, start : start + block_slots]
                    ret_out[m] = jnp.concatenate([part, blank], axis=0).astype(kind)
                for m in range(half * EXP, half * EXP + EXP):

                    @pl.when(back_is_mine(m))
                    def _():
                        ret_in[z % 2, exp] = ret_out[m]

                    @pl.when(jnp.logical_not(back_is_mine(m)))
                    def _():
                        back_copy(m).start()

    gather.drain()
    spread.drain()
    proj_sum.drain()
    for i in range(4):
        pair_copy(i).wait_send()
    for half in BOTH:
        for group in range(5):
            sums[half][group].drain()
    for _, arrive, _ in swaps_share:
        arrive()
    for _, _, drain in swaps_res + swaps_ids + swaps_hid + swaps_share:
        drain()

    @pl.loop(1, EXP)
    def _(k):
        disp_copy(k, exp).wait_send()
        scale_copy(k, exp).wait_send()

    @pl.loop(1, CTX)
    def _(k):
        stat_copy(k, ctx).wait_send()
        state_copy(k, ctx).wait_send()
        prior_copy(k, ctx).wait_send()

    share_col = share_in[0].T
    for i in BOTH:

        @pl.loop(0, EXP)
        def _(k):
            @pl.when(jnp.logical_not(back_from_me(i, k)))
            def _():
                back_arrival(i, k).wait_recv()

        back = ret_in[i].reshape(EXP * BACK, width)
        weighted = [
            (dot(takes[k], back) * share_col[:, k : k + 1]).astype(kind).astype(f32) for k in BOTH
        ]
        mixture_ref[:, i * part_width : (i + 1) * part_width] = (weighted[0] + weighted[1]).astype(
            kind
        )

    @pl.loop(0, 2 * EXP)
    def _(m):
        @pl.when(jnp.logical_not(back_is_mine(m)))
        def _():
            back_copy(m).wait_send()


def layer(query, key, value, decay, residual, out_weight, router, ids, gate_w, up_w, down_w):
    length, inner = query.shape
    head = inner // decay.shape[0]
    width = out_weight.shape[1]
    units, model = down_w.shape
    slots = CTX * (2 * length // EXP + length // 32)
    half_rows = slots // 2
    kind, f32 = query.dtype, jnp.float32
    vmem = pl.BlockSpec(memory_space=pltpu.VMEM)
    anywhere = pl.BlockSpec(memory_space=pl.ANY)
    two = (2, length, width)
    dma = pltpu.SemaphoreType.DMA
    out = jax.ShapeDtypeStruct(residual.shape, kind)
    blocks = (2, 5, 2, slots // SIDE, width)
    return pl.pallas_call(
        layer_kernel,
        out_shape=(out, out),
        in_specs=[vmem] * 8 + [anywhere] * 3,
        out_specs=(vmem, vmem),
        scratch_shapes=[
            pltpu.VMEM((CTX, head // 2 + 16, head), kind),
            pltpu.VMEM((CTX, head // 2 + 16, head), kind),
            pltpu.VMEM((CTX, head // 2, head), kind),
            pltpu.VMEM((CTX, head // 2, head), kind),
            pltpu.VMEM((length, inner), f32),
            pltpu.VMEM((CTX, length, inner), kind),
            pltpu.VMEM((4,) + two, kind),
            pltpu.VMEM((4,) + two, kind),
            pltpu.VMEM(two, kind),
            pltpu.VMEM(two, kind),
            pltpu.VMEM((2,) + two, kind),
            pltpu.VMEM((2,) + two, kind),
            pltpu.VMEM(two, kind),
            pltpu.VMEM(two, kind),
            pltpu.VMEM((8, length), jnp.int32),
            pltpu.VMEM((2, 8, length), jnp.int32),
            pltpu.VMEM(two, kind),
            pltpu.VMEM(two, kind),
            pltpu.VMEM((2, EXP, length), f32),
            pltpu.VMEM((2, EXP, length), f32),
            pltpu.VMEM((EXP, 128, 2 * length), kind),
            pltpu.VMEM((EXP, PAD, width), kind),
            pltpu.VMEM((EXP, PAD, width), kind),
            pltpu.VMEM((2 * EXP, 2 * length), f32),
            pltpu.VMEM((CTX, 2 * EXP, 2 * length), f32),
            pltpu.VMEM((EXP, 8, 128), f32),
            pltpu.VMEM((EXP, 8, 128), f32),
            pltpu.VMEM((slots, 128), f32),
            pltpu.VMEM((2, length, EXP * BACK), kind),
            pltpu.VMEM((CTX, slots, width), kind),
            pltpu.VMEM((2 * units, model), kind),
            pltpu.VMEM((units, model), kind),
            pltpu.VMEM((2, half_rows, 2 * units), f32),
            pltpu.VMEM((slots, units), kind),
            pltpu.VMEM(blocks, kind),
            pltpu.VMEM(blocks, kind),
            pltpu.VMEM((2, 5, 2) + blocks[2:], kind),
            pltpu.VMEM((2, 5, 2) + blocks[2:], kind),
            pltpu.VMEM((2 * EXP, BACK, width), kind),
            pltpu.VMEM((2, EXP, BACK, width), kind),
            dma((3,)), dma((CTX,)), dma((CTX,)), dma((CTX,)), dma((CTX,)), dma((40,)), dma((40,)), dma((40,)), dma((40,)), dma((40,)), dma((40,)),
            dma((4,)), dma((4,)), dma((4,)), dma((4,)), dma((8,)), dma((8,)),
            dma((EXP,)), dma((EXP,)), dma((CTX,)), dma((CTX,)),
            dma((EXP,)), dma((EXP,)), dma((2 * EXP,)), dma((2 * EXP,)),
        ],
        compiler_params=pltpu.CompilerParams(
            collective_id=1, has_side_effects=True, vmem_limit_bytes=62 * 1024 * 1024
        ),
        cost_estimate=pl.CostEstimate(
            flops=6 * slots * model * units, bytes_accessed=6 * model * units, transcendentals=0
        ),
    )(query, key, value, decay, residual, out_weight, router, ids, gate_w, up_w, down_w)


def per_device(
    query_rows,
    key_rows,
    value_rows,
    log_decay,
    residual,
    out_weight,
    router_weight,
    expert_ids,
    expert_gate,
    expert_up,
    expert_down,
):
    return layer(
        query_rows,
        key_rows,
        value_rows,
        log_decay,
        residual,
        out_weight,
        router_weight.T,
        expert_ids.T,
        expert_gate[0].T,
        expert_up[0].T,
        expert_down[0],
    )


def solution(mesh):
    return jax.shard_map(
        per_device,
        mesh=mesh,
        in_specs=(
            P("ctx", "exp"),
            P("ctx", "exp"),
            P("ctx", "exp"),
            P("exp", "ctx"),
            P("ctx", "exp"),
            P("exp", "ctx"),
            P(),
            P("ctx", None),
            P("exp", None, "ctx"),
            P("exp", None, "ctx"),
            P("exp", "ctx", None),
        ),
        out_specs=(P("ctx", "exp"), P("ctx", "exp")),
        check_vma=False,
    )
```

```python
import jax
import jax.numpy as jnp
from jax import lax
from jax.experimental import pallas as pl
from jax.experimental.pallas import tpu as pltpu
from jax.sharding import PartitionSpec as P

MESH = pl.DeviceIdType.MESH
SIDE = 4
CTX = 16
EXP = 8
PAD = 80
BACK = 48
GROUPS = (0, -1, 1, 2)
FAR_FIRST = (2, 1, -1, 0)
STEPS = sorted(
    ((a, b) for a in range(4) for b in range(4) if a or b),
    key=lambda step: -min(step[0], 4 - step[0]) - min(step[1], 4 - step[1]),
)
BOTH = (0, 1)
epsilon = 1e-05
highest = lax.Precision.HIGHEST


def dot(a, b):
    return jnp.dot(a, b, preferred_element_type=jnp.float32)


def dot_rows(a, b):
    return lax.dot_general(a, b, (((1,), (1,)), ((), ())), preferred_element_type=jnp.float32)


def chunk_at(half, u, v):
    u, v = (u + SIDE) % SIDE, (v + SIDE) % SIDE
    return u * SIDE + v if half == 0 else v * SIDE + u


def plane_device(half, axis, step):
    me = lax.axis_index("ctx")
    y, z = me // SIDE, me % SIDE
    u, v = (y, z) if half == 0 else (z, y)
    return chunk_at(half, u + step, v) if axis == 0 else chunk_at(half, u, v + step)


class Gather:
    def __init__(self, buf, send_sem, recv_sem):
        self.buf, self.send_sem, self.recv_sem = buf, send_sem, recv_sem
        self.half_rows = buf.shape[1] // 2
        me = lax.axis_index("ctx")
        y, z = me // SIDE, me % SIDE
        self.place = ((y, z), (z, y))

    def copy(self, half, ring, kind, step):
        u, v = self.place[half]
        axis = 0 if ring == 0 else 1
        held = (0, 0, -1, 1)[kind] + step
        if axis == 0:
            chunk = chunk_at(half, u + held, v)
        else:
            chunk = chunk_at(half, u + GROUPS[ring - 1], v + held)
        start, size = half * self.half_rows, self.half_rows
        if kind >= 2:
            size = size // 2
            start = start + (kind - 2) * size
        ref = self.buf.at[chunk, pl.ds(start, size)]
        k = (half * 5 + ring) * 4 + kind
        return pltpu.make_async_remote_copy(
            src_ref=ref,
            dst_ref=ref,
            send_sem=self.send_sem.at[k],
            recv_sem=self.recv_sem.at[k],
            device_id={"ctx": plane_device(half, axis, 1 if kind % 2 == 0 else -1)},
            device_id_type=MESH,
        )

    def send(self, half, ring, kind):
        self.copy(half, ring, kind, 0).start()

    def arrive(self, half, ring, kind):
        self.copy(half, ring, kind, -1 if kind % 2 == 0 else 1).wait_recv()

    def blocks(self, ring):
        for half in BOTH:
            self.send(half, ring, 0)
            self.send(half, ring, 1)

    def relay(self, ring):
        for half in BOTH:
            self.arrive(half, ring, 0)
            self.send(half, ring, 2)
            self.arrive(half, ring, 1)
            self.send(half, ring, 3)

    def settle(self, ring):
        for half in BOTH:
            self.arrive(half, ring, 2)
            self.arrive(half, ring, 3)

    def drain(self):
        for half in BOTH:
            for ring in range(5):
                for kind in range(4):
                    self.copy(half, ring, kind, 0).wait_send()


class RingSum:
    def __init__(self, rel_out, rel_in, full_out, full_in, send_sem, recv_sem, base, device):
        self.refs = (rel_out, rel_in, full_out, full_in)
        self.send_sem, self.recv_sem, self.base, self.device = send_sem, recv_sem, base, device
    def copy(self, kind):
        rel_out, rel_in, full_out, full_in = self.refs
        if kind < 2:
            src, dst = rel_out.at[kind], rel_in.at[kind]
        else:
            src, dst = full_out.at[kind - 2], full_in.at[kind - 2]
        return pltpu.make_async_remote_copy(
            src_ref=src,
            dst_ref=dst,
            send_sem=self.send_sem.at[self.base + kind],
            recv_sem=self.recv_sem.at[self.base + kind],
            device_id=self.device(1 if kind % 2 == 0 else -1),
            device_id_type=MESH,
        )

    def far(self, value):
        rel_out = self.refs[0]
        rel_out[...] = value.astype(rel_out.dtype)
        self.copy(0).start()
        self.copy(1).start()

    def near(self, way, value):
        _, rel_in, full_out, _ = self.refs
        full_out[way] = value.astype(full_out.dtype)
        self.copy(way).wait_recv()
        full_out[way, way] = (value[way] + rel_in[way].astype(jnp.float32)).astype(full_out.dtype)
        self.copy(2 + way).start()

    def total(self, value):
        full_in = self.refs[3]
        for way in BOTH:
            self.copy(2 + way).wait_recv()
            value = value + full_in[way].astype(jnp.float32)
        return value

    def drain(self):
        for kind in range(4):
            self.copy(kind).wait_send()


def layer_kernel(
    query_ref, key_ref, value_ref, decay_ref,
    residual_ref, out_w, router_ref, ids_ref, gate_hbm, up_hbm, down_hbm,
    result_ref,
    fresh_out, fresh_in, prior_out, prior_in, inside, normed_all, pair_out, pair_in, proj_rel_out, proj_rel_in, proj_full_out, proj_full_in,
    res_out, res_in, ids_out, ids_in, hid_out, hid_in, share_out, share_in,
    picks, disp_out, disp_in, stat_out, stat_in, scale_out, scale_in, scale_col,
    takes, rows, hidden_w, down_w, hidden_acc, active,
    rel_out, rel_in, full_out, full_in, ret_out, ret_in,
    weight_sem, f_send, f_recv, o_send, o_recv, n_send, n_recv, g_send, g_recv, r_send, r_recv, p_send, p_recv, q_send, q_recv,
    swap_send, swap_recv, d_send, d_recv, s_send, s_recv, c_send, c_recv, b_send, b_recv,
):
    ctx, exp = lax.axis_index("ctx"), lax.axis_index("exp")
    y, z = ctx // SIDE, ctx % SIDE
    x, core = exp // 2, exp % 2
    length, part_width = res_in.shape[1], res_in.shape[2]
    width = rows.shape[2]
    slots = rows.shape[1]
    pair_slots = slots // EXP
    half_rows = slots // 2
    model = down_w.shape[1]
    f32, kind = jnp.float32, rows.dtype
    units = down_w.shape[0]
    place = ((y, z), (z, y))

    weight_copies = [
        pltpu.make_async_copy(src, dst, weight_sem.at[i])
        for i, (src, dst) in enumerate(
            (
                (gate_hbm, hidden_w.at[pl.ds(0, units)]),
                (up_hbm, hidden_w.at[pl.ds(units, units)]),
                (down_hbm, down_w),
            )
        )
    ]
    for copy in weight_copies:
        copy.start()

    def partner(i):
        return {"ctx": 2 * exp + i, "exp": ctx // 2}

    def partner_is_me(i):
        return jnp.logical_and(ctx == 2 * exp + i, exp == ctx // 2)

    slot = ctx % 2
    barrier = pltpu.get_barrier_semaphore()

    @pl.loop(1, CTX)
    def _(k):
        pl.semaphore_signal(barrier, inc=1, device_id={"ctx": (ctx + k) % CTX}, device_id_type=MESH)

    @pl.loop(1, EXP)
    def _(k):
        pl.semaphore_signal(barrier, inc=1, device_id={"exp": (exp + k) % EXP}, device_id_type=MESH)

    for i in BOTH:

        @pl.when(jnp.logical_not(partner_is_me(i)))
        def _():
            pl.semaphore_signal(barrier, inc=1, device_id=partner(i), device_id_type=MESH)

    heads = decay_ref.shape[0]
    head = query_ref.shape[1] // heads
    row_index = lax.broadcasted_iota(jnp.int32, (length, length), 0)
    col_index = lax.broadcasted_iota(jnp.int32, (length, length), 1)
    cum_row = jnp.dot(
        decay_ref[...], (row_index <= col_index).astype(f32),
        preferred_element_type=f32, precision=highest,
    )
    cum_col = cum_row.T
    block_total = cum_row[:, length - 1 : length]
    keep = jnp.exp(block_total - cum_row).T
    block_keep = jnp.broadcast_to(jnp.exp(block_total), (heads, head))
    keep_high = block_keep.astype(kind)
    keep_low = (block_keep - keep_high.astype(f32)).astype(kind)
    part_rows = head // 2
    line = lax.broadcasted_iota(jnp.int32, (16, head), 0)
    for h in range(heads):
        lanes = slice(h * head, (h + 1) * head)
        weighted = (key_ref[:, lanes].astype(f32) * keep[:, h : h + 1]).astype(kind)
        state = lax.dot_general(
            weighted, value_ref[:, lanes], (((0,), (0,)), ((), ())), preferred_element_type=f32
        ).astype(kind)
        factor = jnp.where(
            line == 0, keep_high[h : h + 1].astype(f32),
            jnp.where(line == 1, keep_low[h : h + 1].astype(f32), 0.0),
        ).astype(kind)
        for i in BOTH:
            fresh_out[2 * h + i, 0:part_rows] = state[i * part_rows : (i + 1) * part_rows]
            fresh_out[2 * h + i, part_rows : part_rows + 16] = factor
    def back_origin(i, k):
        return {"ctx": y * SIDE + 2 * core + i, "exp": k}

    def back_from_me(i, k):
        return jnp.logical_and(2 * core + i == z, k == exp)

    for i in BOTH:

        @pl.loop(0, EXP)
        def _(k):
            @pl.when(jnp.logical_not(back_from_me(i, k)))
            def _():
                pl.semaphore_signal(barrier, inc=1, device_id=back_origin(i, k), device_id_type=MESH)

    ids_out[0:2, :] = ids_ref[...]
    for i in BOTH:
        res_out[i] = residual_ref[:, i * part_width : (i + 1) * part_width]
    pl.semaphore_wait(
        barrier,
        CTX + EXP - 2 + jnp.where(exp == ctx // 2, 1, 2) + jnp.where(z // 2 == core, 15, 16),
    )

    def swap(index, i, src, dst, mine):
        def copy(arriving):
            k = 2 * index
            return pltpu.make_async_remote_copy(
                src_ref=src,
                dst_ref=dst.at[i] if arriving else dst.at[slot],
                send_sem=swap_send.at[k + i],
                recv_sem=swap_recv.at[k + i] if arriving else swap_recv.at[k + slot],
                device_id=partner(i),
                device_id_type=MESH,
            )

        def start():
            @pl.when(partner_is_me(i))
            def _():
                mine()

            @pl.when(jnp.logical_not(partner_is_me(i)))
            def _():
                copy(False).start()

        def arrive():
            @pl.when(jnp.logical_not(partner_is_me(i)))
            def _():
                copy(True).wait_recv()

        def drain():
            @pl.when(jnp.logical_not(partner_is_me(i)))
            def _():
                copy(False).wait_send()

        return start, arrive, drain

    def stay(src, i, dst):
        def mine():
            dst[i] = src[i]

        return mine

    def stay_ids(i):
        def mine():
            ids_in[i] = ids_out[...]

        return mine

    def ctx_at(step, way):
        return (y + way * step[0] + SIDE) % SIDE * SIDE + (z + way * step[1] + SIDE) % SIDE

    def state_copy(step, src_ctx):
        return pltpu.make_async_remote_copy(
            src_ref=fresh_out.at[ctx_at(step, 1)],
            dst_ref=fresh_in.at[src_ctx],
            send_sem=f_send.at[step[0] * SIDE + step[1]],
            recv_sem=f_recv.at[step[0] * SIDE + step[1]],
            device_id={"ctx": ctx_at(step, 1)},
            device_id_type=MESH,
        )

    def prior_copy(step, src_ctx):
        return pltpu.make_async_remote_copy(
            src_ref=prior_out.at[ctx_at(step, 1)],
            dst_ref=prior_in.at[src_ctx],
            send_sem=o_send.at[step[0] * SIDE + step[1]],
            recv_sem=o_recv.at[step[0] * SIDE + step[1]],
            device_id={"ctx": ctx_at(step, 1)},
            device_id_type=MESH,
        )

    for step in STEPS:
        state_copy(step, ctx).start()

    swaps_res = [swap(0, i, res_out.at[i], res_in, stay(res_out, i, res_in)) for i in BOTH]
    swaps_ids = [swap(1, i, ids_out, ids_in, stay_ids(i)) for i in BOTH]
    for start, _, _ in swaps_ids:
        start()
    fresh_in[ctx] = fresh_out[ctx]
    for h in range(heads):
        lanes = slice(h * head, (h + 1) * head)
        scores = dot_rows(query_ref[:, lanes], key_ref[:, lanes])
        gaps = cum_col[:, h : h + 1] - cum_row[h : h + 1, :]
        decayed = jnp.where(col_index <= row_index, jnp.exp(jnp.minimum(gaps, 0.0)), 0.0)
        inside[:, lanes] = dot((scores * decayed).astype(kind), value_ref[:, lanes])

    for step in STEPS:
        state_copy(step, ctx_at(step, -1)).wait_recv()

    state = jnp.zeros((part_rows, head), f32)
    for j in range(CTX):
        prior_out[j] = state.astype(kind)
        if j < CTX - 1:
            factor = fresh_in[j, part_rows : part_rows + 16].astype(f32)
            state = (factor[0:1] + factor[1:2]) * state + fresh_in[j, 0:part_rows].astype(f32)

    for step in STEPS:
        prior_copy(step, ctx).start()

    prior_in[ctx] = prior_out[ctx]
    grown = jnp.exp(cum_col)
    hidden_acc[...] = jnp.zeros_like(hidden_acc)

    expert_row = lax.broadcasted_iota(jnp.int32, (EXP, length), 0)
    later = (
        lax.broadcasted_iota(jnp.int32, (length, length), 0)
        < lax.broadcasted_iota(jnp.int32, (length, length), 1)
    ).astype(jnp.bfloat16)

    def slots_of(ids):
        chosen = [expert_row == ids[k : k + 1, :] for k in BOTH]
        count = chosen[0].astype(f32) + chosen[1].astype(f32)
        return chosen, count, dot(count.astype(jnp.bfloat16), later)

    chosen, _, before = slots_of(ids_ref[...])
    first_back = before + (expert_row * BACK).astype(f32)
    spot = [jnp.sum(jnp.where(pick, first_back, 0.0), axis=0, keepdims=True) for pick in chosen]
    spot_col = jnp.where(expert_row == 0, spot[0], jnp.where(expert_row == 1, spot[1], 0.0)).T
    back_row = lax.broadcasted_iota(jnp.int32, (length, EXP * BACK), 1).astype(f32)
    for k in BOTH:
        takes[k] = jnp.where(back_row == spot_col[:, k : k + 1], 1.0, 0.0).astype(kind)

    for step in STEPS:
        prior_copy(step, ctx_at(step, -1)).wait_recv()

    for h in range(heads):
        lanes = slice(h * head, (h + 1) * head)
        before_block = prior_in[2 * h : 2 * h + 2].reshape(head, head)
        attended = inside[:, lanes] + dot(query_ref[:, lanes], before_block) * grown[:, h : h + 1]
        square = jnp.mean(attended * attended, axis=1, keepdims=True)
        normed_all[ctx, :, lanes] = (attended * lax.rsqrt(square + epsilon)).astype(kind)

    gather = Gather(normed_all, n_send, n_recv)
    gather.blocks(0)
    gather.blocks(1)
    gather.relay(0)
    gather.blocks(2)
    gather.blocks(3)
    gather.settle(0)
    gather.blocks(4)
    for ring in range(1, 5):
        gather.relay(ring)
    for start, _, _ in swaps_res:
        start()
    for _, arrive, _ in swaps_ids:
        arrive()

    named = []
    for i in BOTH:
        chosen, count, before = slots_of(ids_in[i])
        key = jnp.where(count > 0.5, before + float(i * (pair_slots // 2)), -1.0)
        named.append((key, chosen))
    key = jnp.concatenate([named[0][0], named[1][0]], axis=1)
    slot_row = lax.broadcasted_iota(jnp.int32, (128, 2 * length), 0).astype(f32)
    for e in range(EXP):
        picks[e] = jnp.where(slot_row == key[e : e + 1, :], 1.0, 0.0).astype(picks.dtype)

    for ring in range(1, 5):
        gather.settle(ring)

    def project(x_to, core_to):
        blocks = normed_all[pl.ds(2 * (x_to * 2 + core_to), 2)]
        return dot(blocks.reshape(2 * length, blocks.shape[2]), out_w[...]).reshape(
            2, length, width
        )

    def pair_copy(i):
        return pltpu.make_async_remote_copy(
            src_ref=pair_out.at[i],
            dst_ref=pair_in.at[i],
            send_sem=p_send.at[i],
            recv_sem=p_recv.at[i],
            device_id={"exp": x * 2 + 1 - core},
            device_id_type=MESH,
        )

    for i, step in enumerate(FAR_FIRST):
        pair_out[i] = project((x + step + SIDE) % SIDE, 1 - core).astype(kind)
        pair_copy(i).start()
    proj_sum = RingSum(
        proj_rel_out, proj_rel_in, proj_full_out, proj_full_in, q_send, q_recv, 0,
        lambda step: {"exp": ((x + step + SIDE) % SIDE) * 2 + core},
    )
    for i, step in enumerate(FAR_FIRST):
        value = project((x + step + SIDE) % SIDE, core)
        pair_copy(i).wait_recv()
        value = value + pair_in[i].astype(f32)
        if i == 0:
            proj_sum.far(value)
        elif i < 3:
            proj_sum.near(i - 1, value)
        else:
            value = proj_sum.total(value)
    for _, arrive, _ in swaps_res:
        arrive()
    hid_out[...] = (res_in[...].astype(f32) + value).astype(kind)
    hid = hid_out[...].reshape(2 * length, width)

    def disp_copy(k, src_exp):
        return pltpu.make_async_remote_copy(
            src_ref=disp_out.at[(exp + k) % EXP],
            dst_ref=disp_in.at[src_exp],
            send_sem=d_send.at[k],
            recv_sem=d_recv.at[k],
            device_id={"exp": (exp + k) % EXP},
            device_id_type=MESH,
        )

    for k in (4, 3, 5, 2, 6, 7, 1):
        to = (exp + k) % EXP
        disp_out[to] = dot(picks[to, pl.ds(0, PAD), :], hid).astype(kind)
        disp_copy(k, exp).start()

    swaps_hid = [swap(2, i, hid_out.at[i], hid_in, stay(hid_out, i, hid_in)) for i in BOTH]
    for start, _, _ in swaps_hid:
        start()
    disp_in[exp] = dot(picks[exp, pl.ds(0, PAD), :], hid).astype(kind)

    @pl.loop(1, EXP)
    def _(k):
        disp_copy(k, (exp + EXP - k) % EXP).wait_recv()

    rows[ctx] = (
        disp_in[...].astype(f32)[:, :pair_slots, :].reshape(slots, width).astype(kind)
    )

    def multiply(group, halves=BOTH):
        for half in halves:
            u, v = place[half]
            chunks = [chunk_at(half, u + GROUPS[group], i) for i in range(SIDE)]
            part_rows = pl.ds(half * half_rows, half_rows)
            left = [rows[chunk, part_rows, :] for chunk in chunks]
            right = [
                hidden_w[:, pl.ds(pl.multiple_of(chunk * width, width), width)] for chunk in chunks
            ]
            hidden_acc[half] += dot_rows(
                jnp.concatenate(left, axis=1), jnp.concatenate(right, axis=1)
            )

    spread = Gather(rows, g_send, g_recv)
    spread.blocks(0)
    spread.blocks(1)

    wide = hid.astype(f32)
    columns = pl.ds(pl.multiple_of(ctx * width, width), width)
    stat_out[pl.ds(0, EXP), :] = dot_rows(router_ref[:, columns], hid)
    square = jnp.sum(wide * wide, axis=1, keepdims=True)
    stat_out[pl.ds(EXP, EXP), :] = jnp.broadcast_to(square, (2 * length, 128)).T[:EXP]
    stat_in[ctx] = stat_out[...]

    def stat_copy(k, src_ctx):
        return pltpu.make_async_remote_copy(
            src_ref=stat_out,
            dst_ref=stat_in.at[src_ctx],
            send_sem=s_send.at[k],
            recv_sem=s_recv.at[k],
            device_id={"ctx": (ctx + k) % CTX},
            device_id_type=MESH,
        )

    @pl.loop(1, CTX)
    def _(k):
        stat_copy(k, ctx).start()

    spread.relay(0)
    spread.settle(0)
    spread.blocks(2)
    spread.relay(1)
    spread.blocks(3)

    weight_copies[0].wait()
    weight_copies[1].wait()
    spread.settle(1)
    spread.relay(2)
    multiply(0)
    spread.blocks(4)
    @pl.loop(1, CTX)
    def _(k):
        stat_copy(k, (ctx + CTX - k) % CTX).wait_recv()

    stats = stat_in[0]
    for k in range(1, CTX):
        stats = stats + stat_in[k]
    row_scale = lax.rsqrt(stats[EXP:, :] * (1.0 / model) + epsilon)
    logits = stats[:EXP, :] * row_scale
    high = row_scale.astype(jnp.bfloat16).astype(f32)
    middle = (row_scale - high).astype(jnp.bfloat16).astype(f32)
    low = row_scale - high - middle
    which = lax.broadcasted_iota(jnp.int32, row_scale.shape, 0)
    thirds = jnp.where(
        which == 0, high, jnp.where(which == 1, middle, jnp.where(which == 2, low, 0.0))
    ).astype(jnp.bfloat16)

    def scale_copy(k, src_exp):
        return pltpu.make_async_remote_copy(
            src_ref=scale_out.at[(exp + k) % EXP],
            dst_ref=scale_in.at[src_exp],
            send_sem=c_send.at[k],
            recv_sem=c_recv.at[k],
            device_id={"exp": (exp + k) % EXP},
            device_id_type=MESH,
        )

    slot_scale = dot_rows(thirds, picks[...].reshape(EXP * 128, 2 * length))
    for e in range(EXP):
        scale_out[e] = slot_scale[:, e * 128 : (e + 1) * 128]

    @pl.loop(1, EXP)
    def _(k):
        scale_copy(k, exp).start()

    scale_in[exp] = scale_out[exp]

    picked = []
    for k in BOTH:
        chosen = jnp.concatenate([named[0][1][k], named[1][1][k]], axis=1)
        picked.append(jnp.sum(jnp.where(chosen, logits, 0.0), axis=0, keepdims=True))
    first_weight = 1.0 / (1.0 + jnp.exp(picked[1] - picked[0]))
    second_weight = 1.0 / (1.0 + jnp.exp(picked[0] - picked[1]))
    share = jnp.where(which == 0, first_weight, jnp.where(which == 1, second_weight, 0.0))
    for i in BOTH:
        share_out[i] = share[:, i * length : (i + 1) * length]
    swaps_share = [swap(3, i, share_out.at[i], share_in, stay(share_out, i, share_in)) for i in BOTH]
    for start, _, _ in swaps_share:
        start()

    spread.settle(2)
    spread.relay(3)
    multiply(1)
    spread.settle(3)
    spread.relay(4)
    multiply(2)

    @pl.loop(1, EXP)
    def _(k):
        scale_copy(k, (exp + EXP - k) % EXP).wait_recv()

    row_scales = jnp.sum(scale_in[...], axis=1).T
    for e in range(EXP):
        scale_col[pl.ds(e * pair_slots, pair_slots), :] = jnp.broadcast_to(
            row_scales[:pair_slots, e : e + 1], (pair_slots, 128)
        )
    weight_copies[2].wait()
    spread.settle(4)

    row_blocks = slots // SIDE

    def product(half, du, dv):
        u, v = place[half]
        to = chunk_at(half, u + dv, v + du)
        to_y, to_z = to // SIDE, to % SIDE
        left = active[pl.ds(pl.multiple_of(to_y * row_blocks, 16), row_blocks), :]
        out = []
        for i in BOTH:
            start = pl.multiple_of(((half * 2 + i) * SIDE + to_z) * width, width)
            out.append(dot(left, down_w[:, pl.ds(start, width)]))
        return jnp.stack(out)

    def ring_device(half, axis):
        return lambda step: {"ctx": plane_device(half, axis, step)}

    sums = [
        [
            RingSum(
                rel_out.at[half, group], rel_in.at[half, group],
                full_out.at[half, group], full_in.at[half, group],
                r_send, r_recv, (half * 5 + group) * 4, ring_device(half, 1 if group < 4 else 0),
            )
            for group in range(5)
        ]
        for half in BOTH
    ]

    def back_copy(m):
        to_exp = 2 * (m // SIDE) + z // 2
        return pltpu.make_async_remote_copy(
            src_ref=ret_out.at[m],
            dst_ref=ret_in.at[z % 2, exp],
            send_sem=b_send.at[m],
            recv_sem=b_recv.at[(z % 2) * EXP + exp],
            device_id={"ctx": y * SIDE + m % SIDE, "exp": to_exp},
            device_id_type=MESH,
        )

    def back_arrival(i, k):
        return pltpu.make_async_remote_copy(
            src_ref=ret_out.at[0],
            dst_ref=ret_in.at[i, k],
            send_sem=b_send.at[0],
            recv_sem=b_recv.at[i * EXP + k],
            device_id=back_origin(i, k),
            device_id_type=MESH,
        )

    def back_is_mine(m):
        return jnp.logical_and(m % SIDE == z, 2 * (m // SIDE) + z // 2 == exp)

    for half in BOTH:
        multiply(3, (half,))
        scale = scale_col[pl.ds(half * half_rows, half_rows), 0:1]
        gate = hidden_acc[half, :, :units] * scale
        up = hidden_acc[half, :, units:] * scale
        active[pl.ds(half * half_rows, half_rows), :] = (
            gate * (1.0 / (1.0 + jnp.exp(-gate))) * up
        ).astype(kind)
    for half in BOTH:
        for group in range(4):
            sums[half][group].far(product(half, 2, FAR_FIRST[group]))
    for group in range(4):
        for half in BOTH:
            sums[half][group].near(0, product(half, 1, FAR_FIRST[group]))
            sums[half][group].near(1, product(half, -1, FAR_FIRST[group]))
    for _, arrive, _ in swaps_hid:
        arrive()
    for i in BOTH:
        result_ref[0, :, i * part_width : (i + 1) * part_width] = hid_in[i]
    block_slots = pair_slots // 2
    blank = jnp.zeros((BACK - block_slots, width), f32)
    for group in range(4):
        for half in BOTH:
            value = sums[half][group].total(product(half, 0, FAR_FIRST[group]))
            if group == 0:
                sums[half][4].far(value)
            elif group < 3:
                sums[half][4].near(group - 1, value)
            else:
                value = sums[half][4].total(value)
                for m in range(half * EXP, half * EXP + EXP):
                    start = m % SIDE * block_slots
                    part = value[m // SIDE - 2 * half, start : start + block_slots]
                    ret_out[m] = jnp.concatenate([part, blank], axis=0).astype(kind)
                for m in range(half * EXP, half * EXP + EXP):

                    @pl.when(back_is_mine(m))
                    def _():
                        ret_in[z % 2, exp] = ret_out[m]

                    @pl.when(jnp.logical_not(back_is_mine(m)))
                    def _():
                        back_copy(m).start()

    gather.drain()
    spread.drain()
    proj_sum.drain()
    for i in range(4):
        pair_copy(i).wait_send()
    for half in BOTH:
        for group in range(5):
            sums[half][group].drain()
    for _, arrive, _ in swaps_share:
        arrive()
    for _, _, drain in swaps_res + swaps_ids + swaps_hid + swaps_share:
        drain()

    @pl.loop(1, EXP)
    def _(k):
        disp_copy(k, exp).wait_send()
        scale_copy(k, exp).wait_send()

    @pl.loop(1, CTX)
    def _(k):
        stat_copy(k, ctx).wait_send()

    for step in STEPS:
        state_copy(step, ctx).wait_send()
        prior_copy(step, ctx).wait_send()

    share_col = share_in[0].T
    for i in BOTH:

        @pl.loop(0, EXP)
        def _(k):
            @pl.when(jnp.logical_not(back_from_me(i, k)))
            def _():
                back_arrival(i, k).wait_recv()

        back = ret_in[i].reshape(EXP * BACK, width)
        weighted = [
            (dot(takes[k], back) * share_col[:, k : k + 1]).astype(kind).astype(f32) for k in BOTH
        ]
        result_ref[1, :, i * part_width : (i + 1) * part_width] = (weighted[0] + weighted[1]).astype(
            kind
        )

    @pl.loop(0, 2 * EXP)
    def _(m):
        @pl.when(jnp.logical_not(back_is_mine(m)))
        def _():
            back_copy(m).wait_send()


def layer(query, key, value, decay, residual, out_weight, router, ids, gate_w, up_w, down_w):
    length, inner = query.shape
    head = inner // decay.shape[0]
    width = out_weight.shape[1]
    units, model = down_w.shape
    slots = CTX * (2 * length // EXP + length // 32)
    half_rows = slots // 2
    kind, f32 = query.dtype, jnp.float32
    vmem = pl.BlockSpec(memory_space=pltpu.VMEM)
    anywhere = pl.BlockSpec(memory_space=pl.ANY)
    two = (2, length, width)
    dma = pltpu.SemaphoreType.DMA
    out = jax.ShapeDtypeStruct(residual.shape, kind)
    blocks = (2, 5, 2, slots // SIDE, width)
    results = pl.pallas_call(
        layer_kernel,
        out_shape=jax.ShapeDtypeStruct((2,) + residual.shape, kind),
        in_specs=[vmem] * 8 + [anywhere] * 3,
        out_specs=vmem,
        scratch_shapes=[
            pltpu.VMEM((CTX, head // 2 + 16, head), kind),
            pltpu.VMEM((CTX, head // 2 + 16, head), kind),
            pltpu.VMEM((CTX, head // 2, head), kind),
            pltpu.VMEM((CTX, head // 2, head), kind),
            pltpu.VMEM((length, inner), f32),
            pltpu.VMEM((CTX, length, inner), kind),
            pltpu.VMEM((4,) + two, kind),
            pltpu.VMEM((4,) + two, kind),
            pltpu.VMEM(two, kind),
            pltpu.VMEM(two, kind),
            pltpu.VMEM((2,) + two, kind),
            pltpu.VMEM((2,) + two, kind),
            pltpu.VMEM(two, kind),
            pltpu.VMEM(two, kind),
            pltpu.VMEM((8, length), jnp.int32),
            pltpu.VMEM((2, 8, length), jnp.int32),
            pltpu.VMEM(two, kind),
            pltpu.VMEM(two, kind),
            pltpu.VMEM((2, EXP, length), f32),
            pltpu.VMEM((2, EXP, length), f32),
            pltpu.VMEM((EXP, 128, 2 * length), kind),
            pltpu.VMEM((EXP, PAD, width), kind),
            pltpu.VMEM((EXP, PAD, width), kind),
            pltpu.VMEM((2 * EXP, 2 * length), f32),
            pltpu.VMEM((CTX, 2 * EXP, 2 * length), f32),
            pltpu.VMEM((EXP, 8, 128), f32),
            pltpu.VMEM((EXP, 8, 128), f32),
            pltpu.VMEM((slots, 128), f32),
            pltpu.VMEM((2, length, EXP * BACK), kind),
            pltpu.VMEM((CTX, slots, width), kind),
            pltpu.VMEM((2 * units, model), kind),
            pltpu.VMEM((units, model), kind),
            pltpu.VMEM((2, half_rows, 2 * units), f32),
            pltpu.VMEM((slots, units), kind),
            pltpu.VMEM(blocks, kind),
            pltpu.VMEM(blocks, kind),
            pltpu.VMEM((2, 5, 2) + blocks[2:], kind),
            pltpu.VMEM((2, 5, 2) + blocks[2:], kind),
            pltpu.VMEM((2 * EXP, BACK, width), kind),
            pltpu.VMEM((2, EXP, BACK, width), kind),
            dma((3,)), dma((CTX,)), dma((CTX,)), dma((CTX,)), dma((CTX,)), dma((40,)), dma((40,)), dma((40,)), dma((40,)), dma((40,)), dma((40,)),
            dma((4,)), dma((4,)), dma((4,)), dma((4,)), dma((8,)), dma((8,)),
            dma((EXP,)), dma((EXP,)), dma((CTX,)), dma((CTX,)),
            dma((EXP,)), dma((EXP,)), dma((2 * EXP,)), dma((2 * EXP,)),
        ],
        compiler_params=pltpu.CompilerParams(
            collective_id=1, has_side_effects=True, vmem_limit_bytes=62 * 1024 * 1024
        ),
        cost_estimate=pl.CostEstimate(
            flops=6 * slots * model * units, bytes_accessed=6 * model * units, transcendentals=0
        ),
    )(query, key, value, decay, residual, out_weight, router, ids, gate_w, up_w, down_w)

    def part_results(results_ref, hidden_ref, mixture_ref):
        hidden_ref[...] = results_ref[0]
        mixture_ref[...] = results_ref[1]

    return pl.pallas_call(
        part_results,
        out_shape=(out, out),
        in_specs=[vmem],
        out_specs=(vmem, vmem),
    )(results)


def per_device(
    query_rows,
    key_rows,
    value_rows,
    log_decay,
    residual,
    out_weight,
    router_weight,
    expert_ids,
    expert_gate,
    expert_up,
    expert_down,
):
    return layer(
        query_rows,
        key_rows,
        value_rows,
        log_decay,
        residual,
        out_weight,
        router_weight.T,
        expert_ids.T,
        expert_gate[0].T,
        expert_up[0].T,
        expert_down[0],
    )


def solution(mesh):
    return jax.shard_map(
        per_device,
        mesh=mesh,
        in_specs=(
            P("ctx", "exp"),
            P("ctx", "exp"),
            P("ctx", "exp"),
            P("exp", "ctx"),
            P("ctx", "exp"),
            P("exp", "ctx"),
            P(),
            P("ctx", None),
            P("exp", None, "ctx"),
            P("exp", None, "ctx"),
            P("exp", "ctx", None),
        ),
        out_specs=(P("ctx", "exp"), P("ctx", "exp")),
        check_vma=False,
    )
```
